32 devices in a mesh: seq: 16 (over z, x, core), head: 2 (over y).
Axes of the slice: x: 2, y: 2, z: 4, core: 2. Of those that a mesh axis runs over, the one named last changes fastest.
Arguments:
- queries: bfloat16 [4096, 8192], P('seq', 'head'), may hold values from -4.6 to 4.6
- keys: bfloat16 [4096, 1024], P('seq', 'head'), may hold values from -4.6 to 4.6
- values: bfloat16 [4096, 1024], P('seq', 'head'), may hold values from -4 to 4
- key_keep: int32 [4096], P('seq'), may hold values 0 or 1
- global_positions: int32 [384], replicated, may hold values from 0 to 4095
- gain: bfloat16 [8192], P('head'), may hold values from 0.5 to 1.5
- cotangent: bfloat16 [4096, 8192], P('seq', 'head'), may hold values from -6 to 6
Outputs:
- normed: bfloat16 [4096, 8192], P('seq', 'head')
- query_grad: bfloat16 [4096, 8192], P('seq', 'head')
- key_grad: bfloat16 [4096, 1024], P('seq', 'head')
- value_grad: bfloat16 [4096, 1024], P('seq', 'head')
The draws below stay inside these ranges and needn't reach their ends.
All inputs are finite; a program needn't handle non-finite values. No bound on the sum of `key_keep` on one device may be relied on, other than what follows from the above.
Results may differ from the reference program's by a relative error of at most 0.018.
Values may be sent and summed in bfloat16 or wider, within the bound.
No kernel may reach another device: no remote copies, remote signals or barrier semaphores. Data moves between devices by JAX's collectives and lax.ppermute only.
A program may use at most 64 MiB of HBM per device.

```python
import jax
import jax.numpy as jnp
from jax import lax

QH = 64
KVH = 8
HD = 128
S_DEV = 256
GLOBALS = 384
TOKENS = 4096
LEVELS = 4
N_SEQ = 16


def shared_keys(key):
    entries = jnp.clip(jax.random.normal(jax.random.fold_in(key, 11), (TOKENS, KVH * HD), jnp.float32), -4.0, 4.0)
    return entries


def draw_keys(key, part):
    entries = shared_keys(key)
    return entries.astype(jnp.bfloat16)


def draw_queries(key, part):
    drawn_queries = jnp.clip(jax.random.normal(jax.random.fold_in(key, 21), (TOKENS, QH * HD), jnp.float32), -4.0, 4.0)
    return drawn_queries.astype(jnp.bfloat16)


def draw_values(key, part):
    drawn = jax.random.normal(jax.random.fold_in(key, 31), (TOKENS, KVH * HD), jnp.float32)
    return jnp.clip(drawn, -4.0, 4.0).astype(jnp.bfloat16)


def draw_cotangent(key, part):
    query_all = draw_queries(key, part).astype(jnp.float32)
    key_all = draw_keys(key, part).astype(jnp.float32)
    value_all = draw_values(key, part).astype(jnp.float32)
    shard_count = TOKENS // S_DEV
    group_size = QH // KVH
    key_shards = key_all.reshape(shard_count, S_DEV, KVH * HD)
    value_shards = value_all.reshape(shard_count, S_DEV, KVH * HD)

    def shard_mix(shard_index):
        partners = [shard_index] + [jnp.bitwise_xor(shard_index, 1 << level_bit) for level_bit in range(LEVELS)]
        chosen_ids = jnp.stack(partners).astype(jnp.int32)
        near_keys = key_shards[chosen_ids].reshape(-1, KVH, HD)
        near_values = value_shards[chosen_ids].reshape(-1, KVH, HD)
        start_row = (shard_index * S_DEV).astype(jnp.int32)
        own_queries = lax.dynamic_slice_in_dim(query_all, start_row, S_DEV, 0).reshape(S_DEV, KVH, group_size, HD)
        scores = jnp.einsum('sagd,kad->agsk', own_queries, near_keys) * HD ** (-0.5)
        weights = jax.nn.softmax(scores, -1)
        mixed = jnp.einsum('agsk,kad->sagd', weights, near_values)
        return mixed.reshape(S_DEV, QH * HD)
    attn_guess = lax.map(shard_mix, jnp.arange(shard_count, dtype=jnp.int32)).reshape(TOKENS, QH * HD)
    direction = attn_guess * lax.rsqrt(jnp.mean(attn_guess * attn_guess, -1, keepdims=True) + 1e-06)
    noise = jnp.clip(jax.random.normal(jax.random.fold_in(key, 41), (TOKENS, QH * HD), jnp.float32), -4.0, 4.0)
    strength = jax.random.uniform(jax.random.fold_in(key, 42), (TOKENS, 1), jnp.float32, 0.5, 1.5)
    return jnp.clip(noise + strength * direction, -6.0, 6.0).astype(jnp.bfloat16)


def set_ends(values, key, smallest, top_value):
    shape = values.shape
    index_at = [jax.random.randint(jax.random.fold_in(key, axis), (), 0, shape[axis]) for axis in range(len(shape))]
    values = values.at[tuple(index_at)].set(smallest)
    longest = shape.index(max(shape))
    index_at[longest] = (index_at[longest] + 1) % shape[longest]
    return values.at[tuple(index_at)].set(top_value)


def setup_inputs(seed: int = 0) -> dict:
    splits = jax.random.split(jax.random.key(seed), 8)
    queries = draw_queries(jax.random.fold_in(splits[7], 71), 0)
    keys = draw_keys(jax.random.fold_in(splits[7], 71), 0)
    values = draw_values(jax.random.fold_in(splits[7], 71), 0)
    key_keep = set_ends((jax.random.randint(splits[3], (TOKENS,), 0, 8) < 7).astype(jnp.int32), jax.random.fold_in(splits[3], 1), 0, 1)
    global_positions = set_ends(jax.random.randint(splits[4], (GLOBALS,), 0, TOKENS), jax.random.fold_in(splits[4], 1), 0, TOKENS - 1).astype(jnp.int32)
    gain = jnp.clip(1.0 + 0.1 * jax.random.normal(splits[5], (QH * HD,), jnp.float32), 0.5, 1.5).astype(jnp.bfloat16)
    cotangent = draw_cotangent(jax.random.fold_in(splits[7], 71), 0)
    return dict(queries=queries, keys=keys, values=values, key_keep=key_keep, global_positions=global_positions, gain=gain, cotangent=cotangent)


NEG_FILL = -1e+30
NORM_EPS = 1e-06

def shard_terms(shard_index, queries, keys, values, key_keep, global_positions, gain, cotangent):
    feature_width = KVH * HD
    group_size = QH // KVH
    scaling = HD ** (-0.5)
    offset_rows = (shard_index * S_DEV).astype(jnp.int32)
    own_queries = lax.dynamic_slice_in_dim(queries, offset_rows, S_DEV, 0)
    own_cotangent = lax.dynamic_slice_in_dim(cotangent, offset_rows, S_DEV, 0)
    own_keep = lax.dynamic_slice_in_dim(key_keep, offset_rows, S_DEV, 0)
    key_blocks = [lax.dynamic_slice_in_dim(keys, offset_rows, S_DEV, 0)]
    value_blocks = [lax.dynamic_slice_in_dim(values, offset_rows, S_DEV, 0)]
    masks = [(own_keep[None, :] == 1) | jnp.eye(S_DEV, dtype=bool)]
    for level_bit in range(LEVELS):
        partner_rows = (jnp.bitwise_xor(shard_index, 1 << level_bit) * S_DEV).astype(jnp.int32)
        key_blocks.append(lax.dynamic_slice_in_dim(keys, partner_rows, S_DEV, 0))
        value_blocks.append(lax.dynamic_slice_in_dim(values, partner_rows, S_DEV, 0))
        partner_keep = lax.dynamic_slice_in_dim(key_keep, partner_rows, S_DEV, 0)
        masks.append(jnp.broadcast_to(partner_keep[None, :] == 1, (S_DEV, S_DEV)))
    key_blocks.append(keys[global_positions])
    value_blocks.append(values[global_positions])
    masks.append(jnp.broadcast_to(key_keep[global_positions][None, :] == 1, (S_DEV, GLOBALS)))
    all_keys = jnp.concatenate(key_blocks, 0)
    all_values = jnp.concatenate(value_blocks, 0)
    visible = jnp.concatenate(masks, 1)
    slots = all_keys.shape[0]
    query_heads = own_queries.reshape(S_DEV, KVH, group_size, HD).astype(jnp.float32)
    key_heads = all_keys.reshape(slots, KVH, HD).astype(jnp.float32)
    value_heads = all_values.reshape(slots, KVH, HD).astype(jnp.float32)
    scores = jnp.einsum('sagd,kad->agsk', query_heads, key_heads) * scaling
    scores = jnp.where(visible[None, None], scores, NEG_FILL)
    peak = lax.optimization_barrier(jnp.max(scores, -1, keepdims=True))
    expo = jnp.exp(scores - peak)
    total = lax.optimization_barrier(jnp.sum(expo, -1, keepdims=True))
    expo_bf = expo.astype(jnp.bfloat16).astype(jnp.float32)
    mixed = jnp.einsum('agsk,kad->agsd', expo_bf, value_heads) / total
    attn = jnp.transpose(mixed, (2, 0, 1, 3)).reshape(S_DEV, QH * HD)
    feature_count = QH * HD
    squares = lax.optimization_barrier(jnp.sum(attn * attn, -1))
    inverse = lax.rsqrt(squares / feature_count + NORM_EPS)
    gain_wide = gain.astype(jnp.float32)
    normed = (attn * inverse[:, None] * gain_wide).astype(jnp.bfloat16)
    upstream = own_cotangent.astype(jnp.float32) * gain_wide
    crossed = lax.optimization_barrier(jnp.sum(upstream * attn, -1))
    d_attn = inverse[:, None] * upstream - attn * (inverse ** 3 * crossed / feature_count)[:, None]
    d_attn_bf = d_attn.astype(jnp.bfloat16).astype(jnp.float32)
    d_heads = d_attn.reshape(S_DEV, KVH, group_size, HD)
    d_heads_bf = d_attn_bf.reshape(S_DEV, KVH, group_size, HD)
    attn_heads = attn.reshape(S_DEV, KVH, group_size, HD)
    probs = expo / total
    d_probs = jnp.einsum('sagd,kad->agsk', d_heads_bf, value_heads)
    diag_term = jnp.einsum('sagd,sagd->ags', d_heads, attn_heads)[..., None]
    d_scores = (probs * (d_probs - diag_term)).astype(jnp.bfloat16).astype(jnp.float32)
    probs_bf = probs.astype(jnp.bfloat16).astype(jnp.float32)
    d_query = jnp.einsum('agsk,kad->sagd', d_scores, key_heads) * scaling
    d_query = d_query.reshape(S_DEV, QH * HD).astype(jnp.bfloat16)
    d_key = (jnp.einsum('agsk,sagd->kad', d_scores, query_heads) * scaling).reshape(slots, feature_width)
    d_value = jnp.einsum('agsk,sagd->kad', probs_bf, d_heads_bf).reshape(slots, feature_width)
    return (normed, d_query, d_key, d_value)

def spread_back(slot_grads, global_positions):
    running = slot_grads[:, :S_DEV]
    shard_ids = jnp.arange(N_SEQ, dtype=jnp.int32)
    for level_bit in range(LEVELS):
        block = slot_grads[:, S_DEV * (level_bit + 1):S_DEV * (level_bit + 2)]
        running = running + block[jnp.bitwise_xor(shard_ids, 1 << level_bit)]
    global_sum = lax.optimization_barrier(jnp.sum(slot_grads[:, S_DEV * (LEVELS + 1):], 0))
    running = running.reshape(TOKENS, KVH * HD).at[global_positions].add(global_sum)
    return running.astype(jnp.bfloat16)

def reference(queries, keys, values, key_keep, global_positions, gain, cotangent):

    def per_shard(shard_index):
        return shard_terms(shard_index, queries, keys, values, key_keep, global_positions, gain, cotangent)
    normed, query_grad, key_slots, value_slots = lax.map(per_shard, jnp.arange(N_SEQ, dtype=jnp.int32))
    normed = normed.reshape(TOKENS, QH * HD)
    query_grad = query_grad.reshape(TOKENS, QH * HD)
    key_grad = spread_back(key_slots, global_positions)
    value_grad = spread_back(value_slots, global_positions)
    return (normed, query_grad, key_grad, value_grad)
```

```python
import functools
import math

import jax
import jax.numpy as jnp
from jax import lax
from jax.experimental import pallas as pl
from jax.experimental.pallas import tpu as pltpu
from jax.sharding import PartitionSpec as P

QH = 64
KVH = 8
HD = 128
GROUP = QH // KVH

NEG_FILL = -1e30
NORM_EPS = 1e-06
HIDDEN = 256.0
HIDDEN_ABOVE = 100.0
SCALING = HD ** (-0.5)
EXPONENT = SCALING * math.log2(math.e)
VMEM_BYTES = 56 * 2**20

F32 = jnp.float32
BF16 = jnp.bfloat16


def dot_nt(left, right):
    return lax.dot_general(left, right, (((1,), (1,)), ((), ())), preferred_element_type=F32)


def dot_nn(left, right):
    return lax.dot_general(left, right, (((1,), (0,)), ((), ())), preferred_element_type=F32)


def dot_tn(left, right):
    return lax.dot_general(left, right, (((0,), (0,)), ((), ())), preferred_element_type=F32)


def swap(block, axis, mask):
    count = lax.axis_size(axis)
    return lax.ppermute(block, axis, [(i, i ^ mask) for i in range(count)])


def params():
    return pltpu.CompilerParams(vmem_limit_bytes=VMEM_BYTES)


def cost(flops, moved, expos=0):
    return pl.CostEstimate(flops=int(flops), bytes_accessed=int(moved), transcendentals=int(expos))


def lane_of(shape):
    return lax.broadcasted_iota(jnp.int32, shape, 1)


def read_global(refs, core_ref):
    count = len(refs) // 2
    mine = jnp.concatenate([r[...] for r in refs[:count]], 0)
    other = jnp.concatenate([r[...] for r in refs[count:]], 0)
    first = core_ref[0] == 0
    return jnp.where(first, mine, other), jnp.where(first, other, mine)


def forward_kernel(blocks, own, is_global, first, last, *refs):
    refs = list(refs)
    take = refs.pop
    q_ref = take(0)
    if is_global:
        core_ref = take(0)
        parts = [take(0) for _ in range(blocks)]
        key_list, value_list = [[x] for x in read_global(parts, core_ref)]
    else:
        key_list, value_list = [], []
        for _ in range(blocks):
            key_list.append(take(0)[...])
            value_list.append(take(0)[...])
    bias_ref = take(0) if own else None
    if not first:
        sum_ref, peak_ref, total_ref = take(0), take(0), take(0)
    if last:
        cot_ref, gain_ref = take(0), take(0)
    p_ref, out_ref, peak_out, total_out = take(0), take(0), take(0), take(0)
    if last:
        rows_ref, square_acc, cross_acc = take(0), take(0), take(0)
        step = pl.program_id(0)

        @pl.when(step == 0)
        def _():
            square_acc[...] = jnp.zeros_like(square_acc)
            cross_acc[...] = jnp.zeros_like(cross_acc)

    rows = q_ref.shape[0]
    unit = (lane_of((rows, HD)) == 0).astype(BF16)
    lanes = lane_of((rows, HD))
    wide_keys, wide_values = [], []
    for number, (k, v) in enumerate(zip(key_list, value_list)):
        if own and number == 0:
            extra = jnp.zeros_like(k)
        else:
            hidden = (lane_of(k.shape) == 0) & (k.astype(F32) > HIDDEN_ABOVE)
            extra = jnp.where(hidden, NEG_FILL, 0.0).astype(BF16)
        wide_keys.append(jnp.concatenate([k, extra], 1))
        wide_values.append(jnp.concatenate([v, jnp.ones_like(v)], 1))

    def scores_of(head):
        q = jnp.concatenate([q_ref[:, head * HD : (head + 1) * HD], unit], 1)
        out = []
        for number, k in enumerate(wide_keys):
            s = dot_nt(q, k)
            if own and number == 0:
                s = s + bias_ref[...]
            out.append(s)
        return out

    peaks = jnp.zeros((rows, HD), F32)
    totals = jnp.ones((rows, HD), F32)
    ahead = scores_of(0)
    for head in range(GROUP):
        scores = ahead
        if head + 1 < GROUP:
            ahead = scores_of(head + 1)
        peak = functools.reduce(
            jnp.maximum, [jnp.max(s, -1, keepdims=True) for s in scores]
        )
        if not first:
            before = peak_ref[:, head : head + 1]
            peak = jnp.maximum(peak, before)
        mixed = None
        start = 0
        for s, v in zip(scores, wide_values):
            e = jnp.exp2((s - peak) * EXPONENT).astype(BF16)
            p_ref[head * rows : (head + 1) * rows, start : start + s.shape[1]] = e
            start += s.shape[1]
            part = dot_nn(e, v)
            mixed = part if mixed is None else mixed + part
        value_sum = mixed[:, :HD]
        total = mixed[:, HD:]
        here = slice(head * HD, (head + 1) * HD)
        if not first:
            shrink = jnp.exp2((before - peak) * EXPONENT)
            value_sum = value_sum + sum_ref[:, here] * shrink
            total = total + total_ref[:, head : head + 1] * shrink
        if last:
            inverse_total = 1.0 / total
            attn = value_sum * inverse_total
            out_ref[:, here] = attn
            totals = jnp.where(lanes == head, inverse_total, totals)
            upstream = cot_ref[:, here].astype(F32) * gain_ref[:, here].astype(F32)
            square_acc[...] += attn * attn
            cross_acc[...] += upstream * attn
        else:
            out_ref[:, here] = value_sum
            totals = jnp.where(lanes == head, total, totals)
        peaks = jnp.where(lanes == head, peak, peaks)
    peak_out[...] = peaks
    total_out[...] = totals
    if last:

        @pl.when(step == pl.num_programs(0) - 1)
        def _():
            squares = jnp.sum(square_acc[...].T, 0, keepdims=True)
            crosses = jnp.sum(cross_acc[...].T, 0, keepdims=True)
            rows_ref[...] = jnp.concatenate([squares, crosses], 0)


def column_block(rows, width):
    return pl.BlockSpec((rows, width), lambda a: (0, a))


def fixed_block(shape):
    return pl.BlockSpec(shape, lambda a: (0,) * len(shape))


SCALAR = pl.BlockSpec(memory_space=pltpu.SMEM)


def forward_phase(name, queries, pairs, core=None, bias=None, before=None, norm=None):
    rows, width = queries.shape
    steps = width // (GROUP * HD)
    wide = GROUP * HD
    args, specs = [queries], [column_block(rows, wide)]
    is_global = core is not None
    if is_global:
        args.append(core)
        specs.append(SCALAR)
        flat = pairs
        slots = sum(x.shape[0] for x in pairs) // 2
    else:
        flat = [x for pair in pairs for x in pair]
        slots = sum(k.shape[0] for k, _ in pairs)
    for x in flat:
        args.append(x)
        specs.append(column_block(x.shape[0], HD))
    if bias is not None:
        args.append(bias)
        specs.append(fixed_block(bias.shape))
    if before is not None:
        args += list(before)
        specs += [column_block(rows, wide), column_block(rows, HD), column_block(rows, HD)]
    if norm is not None:
        cotangent, gain = norm
        args += [cotangent, gain]
        specs += [column_block(rows, wide), column_block(1, wide)]
    out_shapes = [
        jax.ShapeDtypeStruct((steps * GROUP * rows, slots), BF16),
        jax.ShapeDtypeStruct((rows, width), F32),
        jax.ShapeDtypeStruct((rows, steps * HD), F32),
        jax.ShapeDtypeStruct((rows, steps * HD), F32),
    ]
    out_specs = [
        pl.BlockSpec((GROUP * rows, slots), lambda a: (a, 0)),
        column_block(rows, wide),
        column_block(rows, HD),
        column_block(rows, HD),
    ]
    scratch = []
    if norm is not None:
        out_shapes.append(jax.ShapeDtypeStruct((2, rows), F32))
        out_specs.append(fixed_block((2, rows)))
        scratch = [pltpu.VMEM((rows, HD), F32), pltpu.VMEM((rows, HD), F32)]
    elements = rows * slots * steps * GROUP
    return pl.pallas_call(
        functools.partial(
            forward_kernel,
            len(pairs),
            bias is not None,
            is_global,
            before is None,
            norm is not None,
        ),
        grid=(steps,),
        in_specs=specs,
        out_specs=out_specs,
        out_shape=out_shapes,
        scratch_shapes=scratch,
        compiler_params=params(),
        cost_estimate=cost(8 * elements * HD, 2 * elements, elements),
        name=name,
    )(*args)


def backward_kernel(blocks, own, is_global, first, last, features, *refs):
    refs = list(refs)
    take = refs.pop
    q_ref, p_ref = take(0), take(0)
    if is_global:
        core_ref = take(0)
        parts = [take(0) for _ in range(blocks)]
        sizes = [r.shape[0] for r in parts[: blocks // 2]]
        key_list, value_list = [[x] for x in read_global(parts, core_ref)]
    else:
        key_list, value_list = [], []
        for _ in range(blocks):
            key_list.append(take(0)[...])
            value_list.append(take(0)[...])
    peak_ref, last_peak_ref, inverse_ref = take(0), take(0), take(0)
    if first:
        norm_ref, attn_ref, cot_ref, gain_ref = take(0), take(0), take(0), take(0)
    else:
        grad_ref, diag_ref, dq_ref = take(0), take(0), take(0)
    outs = [take(0) for _ in range(blocks if is_global else 2 * blocks)]
    dq_out = take(0)
    if first:
        normed_out, grad_out, diag_out = take(0), take(0), take(0)
    ds_ref, q_stack, grad_stack = take(0), take(0), take(0)

    rows = q_ref.shape[0]
    lanes = lane_of((rows, HD))
    factors = jnp.exp2((peak_ref[...] - last_peak_ref[...]) * EXPONENT) * inverse_ref[...]
    if first:
        squares = norm_ref[0:1, :]
        crossed = norm_ref[1:2, :]
        inverse_row = lax.rsqrt(squares / features + NORM_EPS)
        coefficient_row = inverse_row * inverse_row * inverse_row * crossed / features
        inverse_wide = jnp.broadcast_to(inverse_row, (HD, rows)).T
        coefficient_wide = jnp.broadcast_to(coefficient_row, (HD, rows)).T
        diags = jnp.zeros((rows, HD), F32)
    for head in range(GROUP):
        here = slice(head * HD, (head + 1) * HD)
        stack = slice(head * rows, (head + 1) * rows)
        factor = factors[:, head : head + 1]
        if first:
            attn = attn_ref[:, here]
            gain = gain_ref[:, here].astype(F32)
            normed_out[:, here] = (attn * inverse_wide * gain).astype(BF16)
            upstream = cot_ref[:, here].astype(F32) * gain
            grad = inverse_wide * upstream - attn * coefficient_wide
            grad_out[:, here] = grad
            diag = jnp.sum(grad * attn, -1, keepdims=True)
            diags = jnp.where(lanes == head, diag, diags)
        else:
            grad = grad_ref[:, here]
            diag = diag_ref[:, head : head + 1]
        grad_bf = (grad * factor).astype(BF16)
        scaled_diag = diag * factor
        grad_stack[stack, :] = grad_bf
        q_stack[stack, :] = q_ref[:, here]
        start = 0
        d_query = None
        for k, v in zip(key_list, value_list):
            columns = slice(start, start + k.shape[0])
            d_probs = dot_nt(grad_bf, v)
            d_scores = (p_ref[stack, columns].astype(F32) * (d_probs - scaled_diag)).astype(BF16)
            ds_ref[stack, columns] = d_scores
            part = dot_nn(d_scores, k)
            d_query = part if d_query is None else d_query + part
            start += k.shape[0]
        if not first:
            d_query = d_query + dq_ref[:, here]
        if last:
            d_query = d_query * SCALING
        dq_out[:, here] = d_query.astype(dq_out.dtype)
    if first:
        diag_out[...] = diags
    q_all, grad_all = q_stack[...], grad_stack[...]
    if is_global:
        d_key = (dot_tn(q_all, ds_ref[...]) * SCALING).T.astype(BF16)
        d_value = dot_tn(grad_all, p_ref[...]).T.astype(BF16)
        core_first = core_ref[0] == 0
        mine = jnp.where(core_first, d_key, d_value)
        other = jnp.where(core_first, d_value, d_key)
        start = 0
        for number, size in enumerate(sizes):
            outs[number][...] = mine[start : start + size]
            outs[number + blocks // 2][...] = other[start : start + size]
            start += size
    else:
        start = 0
        for number, k in enumerate(key_list):
            columns = slice(start, start + k.shape[0])
            start += k.shape[0]
            d_key = (dot_tn(q_all, ds_ref[:, columns]) * SCALING).T
            d_value = dot_tn(grad_all, p_ref[:, columns]).T
            outs[2 * number][...] = d_key.astype(outs[2 * number].dtype)
            outs[2 * number + 1][...] = d_value.astype(outs[2 * number + 1].dtype)


def backward_phase(
    name, queries, probs, pairs, peaks, last_peaks, inverse, own=False, core=None,
    norm=None, grads=None, last=False,
):
    rows, width = queries.shape
    steps = width // (GROUP * HD)
    wide = GROUP * HD
    slots = probs.shape[1]
    args = [queries, probs]
    specs = [column_block(rows, wide), pl.BlockSpec((GROUP * rows, slots), lambda a: (a, 0))]
    is_global = core is not None
    if is_global:
        args.append(core)
        specs.append(SCALAR)
        flat = pairs
    else:
        flat = [x for pair in pairs for x in pair]
    out_shapes, out_specs = [], []
    for number, x in enumerate(flat):
        args.append(x)
        specs.append(column_block(x.shape[0], HD))
        kind = F32 if own and number < 2 else BF16
        out_shapes.append(jax.ShapeDtypeStruct(x.shape, kind))
        out_specs.append(column_block(x.shape[0], HD))
    args += [peaks, last_peaks, inverse]
    specs += [column_block(rows, HD)] * 3
    if norm is not None:
        sums, attn, cotangent, gain = norm
        args += [sums, attn, cotangent, gain]
        specs += [
            fixed_block(sums.shape),
            column_block(rows, wide),
            column_block(rows, wide),
            column_block(1, wide),
        ]
    else:
        args += list(grads)
        specs += [column_block(rows, wide), column_block(rows, HD), column_block(rows, wide)]
    out_shapes.append(jax.ShapeDtypeStruct((rows, width), BF16 if last else F32))
    out_specs.append(column_block(rows, wide))
    if norm is not None:
        out_shapes += [
            jax.ShapeDtypeStruct((rows, width), BF16),
            jax.ShapeDtypeStruct((rows, width), F32),
            jax.ShapeDtypeStruct((rows, steps * HD), F32),
        ]
        out_specs += [
            column_block(rows, wide),
            column_block(rows, wide),
            column_block(rows, HD),
        ]
    elements = rows * slots * steps * GROUP
    return pl.pallas_call(
        functools.partial(
            backward_kernel, len(pairs), own, is_global, norm is not None, last, QH * HD
        ),
        grid=(steps,),
        in_specs=specs,
        out_specs=out_specs,
        out_shape=out_shapes,
        scratch_shapes=[
            pltpu.VMEM((GROUP * rows, slots), BF16),
            pltpu.VMEM((GROUP * rows, HD), BF16),
            pltpu.VMEM((GROUP * rows, HD), BF16),
        ],
        compiler_params=params(),
        cost_estimate=cost(12 * elements * HD, 2 * elements),
        name=name,
    )(*args)


def pick_kernel(core_ref, spots_ref, k_ref, v_ref, pk_ref, pv_ref, out_ref):
    rows = k_ref.shape[0]
    count = spots_ref.shape[1]
    first = core_ref[0] == 0
    row_ids = lax.broadcasted_iota(jnp.int32, (rows, count), 0)
    total = None
    for number, (k, v) in enumerate(((k_ref, v_ref), (pk_ref, pv_ref))):
        source = jnp.where(first, k[...], v[...])
        chosen = jnp.where(row_ids == spots_ref[number : number + 1, :], 1.0, 0.0).astype(BF16)
        part = dot_tn(chosen, source)
        total = part if total is None else total + part
    out_ref[...] = total.astype(BF16)


def pick(core, spots, keys, values, partner_keys, partner_values):
    full = pl.BlockSpec(memory_space=pltpu.VMEM)
    shape = (spots.shape[1], keys.shape[1])
    return pl.pallas_call(
        pick_kernel,
        in_specs=[SCALAR] + [full] * 5,
        out_specs=full,
        out_shape=jax.ShapeDtypeStruct(shape, BF16),
        compiler_params=params(),
        cost_estimate=cost(4 * shape[0] * shape[1] * keys.shape[0], 3 * 2**20),
        name="pick_globals",
    )(core, spots, keys, values, partner_keys, partner_values)


def finish_kernel(partners, parts, *refs):
    core_ref, spots_ref = refs[0], refs[1]
    own = refs[2:4]
    back = refs[4 : 4 + 2 * partners]
    total = refs[4 + 2 * partners : 4 + 2 * partners + 2 * parts]
    outs = refs[4 + 2 * partners + 2 * parts :]
    rows = own[0].shape[0]
    count = spots_ref.shape[1]
    row_ids = lax.broadcasted_iota(jnp.int32, (rows, count), 0)
    chosen = jnp.where(row_ids == spots_ref[0:1, :], 1.0, 0.0).astype(BF16)
    global_grads = read_global(total, core_ref)
    for kind in range(2):
        running = own[kind][...]
        for number in range(partners):
            running = running + back[2 * number + kind][...].astype(F32)
        running = running + dot_nn(chosen, global_grads[kind])
        outs[kind][...] = running.astype(BF16)


def finish(core, spots, own, back, total):
    full = pl.BlockSpec(memory_space=pltpu.VMEM)
    args = list(own) + list(back) + list(total)
    return pl.pallas_call(
        functools.partial(finish_kernel, len(back) // 2, len(total) // 2),
        in_specs=[SCALAR] + [full] * (len(args) + 1),
        out_specs=[full] * 2,
        out_shape=[jax.ShapeDtypeStruct(own[0].shape, BF16)] * 2,
        compiler_params=params(),
        cost_estimate=cost(2**28, 4 * 2**20),
        name="finish_key_value_grads",
    )(core, spots, *args)


def levels_of(bit_count):
    bits = list(range(1, bit_count))
    levels = []
    while bits:
        levels.insert(0, bits[-2:])
        bits = bits[:-2]
    return levels


def masks_of(level):
    return [
        sum(1 << bit for place, bit in enumerate(level) if number >> place & 1)
        for number in range(1 << len(level))
    ]


def reduce_level(block, masks):
    size = block.shape[0] // len(masks)
    running = block[:size].astype(F32)
    for number, mask in enumerate(masks):
        if number:
            moved = swap(block[number * size : (number + 1) * size], "seq", mask)
            running = running + moved.astype(F32)
    return running.astype(BF16)


def gather_level(block, masks):
    return [block if mask == 0 else swap(block, "seq", mask) for mask in masks]


def per_device(queries, keys, values, key_keep, global_positions, gain, cotangent):
    rows = queries.shape[0]
    bit_count = lax.axis_size("seq").bit_length() - 1
    place = lax.axis_index("seq")
    core = (place & 1).reshape(1)
    global_count = global_positions.shape[0]

    marked = jnp.where(key_keep[:, None] == 1, keys, jnp.asarray(HIDDEN, BF16))
    near = [(swap(marked, "seq", 1 << bit), swap(values, "seq", 1 << bit)) for bit in range(bit_count)]

    levels = [masks_of(level) for level in levels_of(bit_count)]
    order = [0]
    for masks in levels:
        order = [base ^ mask for base in order for mask in masks]
    pieces = len(order)
    chunk_ids = (place >> 1) ^ jnp.array([mask >> 1 for mask in order], jnp.int32)
    chunks = global_positions.reshape(pieces, global_count // pieces)
    match = chunk_ids[:, None] == jnp.arange(pieces, dtype=jnp.int32)[None, :]
    ordered = jnp.sum(jnp.where(match[:, :, None], chunks[None], 0), 1).reshape(global_count)
    spots = jnp.stack([ordered - place * rows, ordered - (place ^ 1) * rows])

    picked = pick(core, spots, marked, values, near[0][0], near[0][1])
    for masks in levels:
        picked = reduce_level(picked, masks)
    mine = [picked]
    for masks in reversed(levels):
        block = mine[0] if len(mine) == 1 else jnp.concatenate(mine, 0)
        mine = gather_level(block, masks)
    global_parts = mine + [swap(part, "seq", 1) for part in mine]

    positions = jnp.arange(rows, dtype=jnp.int32)
    visible = (key_keep[None, :] == 1) | (positions[:, None] == positions[None, :])
    bias = jnp.where(visible, 0.0, NEG_FILL).astype(F32)
    gain_row = gain.reshape(1, -1)

    groups = [[(keys, values), near[0]]]
    if bit_count > 2:
        groups.append(near[1:-1])
    if bit_count > 1:
        groups.append(near[-1:])
    state = None
    probs, peaks = [], []
    for number, group in enumerate(groups):
        p, *state = forward_phase(
            f"forward_slots_{number}", queries, group, bias=bias if number == 0 else None, before=state
        )
        probs.append(p)
        peaks.append(state[1])
    p_global, attn, last_peaks, inverse, sums = forward_phase(
        "forward_globals", queries, global_parts, core=core, before=state, norm=(cotangent, gain_row)
    )
    head_bits = lax.axis_size("head").bit_length() - 1
    for bit in range(head_bits):
        sums = sums + swap(sums, "head", 1 << bit)

    *global_grads, d_query, normed, grad, diag = backward_phase(
        "backward_globals", queries, p_global, global_parts, last_peaks, last_peaks, inverse,
        core=core, norm=(sums, attn, cotangent, gain_row),
    )
    half = len(global_grads) // 2
    reduced = [
        (a.astype(F32) + swap(b, "seq", 1).astype(F32)).astype(BF16)
        for a, b in zip(global_grads[:half], global_grads[half:])
    ]
    block = reduced
    for masks in levels:
        running = block[0].astype(F32) if isinstance(block, list) else None
        if isinstance(block, list):
            for part, mask in zip(block[1:], masks[1:]):
                running = running + swap(part, "seq", mask).astype(F32)
            block = running.astype(BF16)
        else:
            block = reduce_level(block, masks)
    mine = [block]
    for masks in reversed(levels):
        block = mine[0] if len(mine) == 1 else jnp.concatenate(mine, 0)
        mine = gather_level(block, masks)
    total_parts = mine + [swap(part, "seq", 1) for part in mine]

    back = []
    own_grads = None
    bits_of = [[0], list(range(1, bit_count - 1)), [bit_count - 1]]
    bits_of = [bits_of[0]] + [b for b in bits_of[1:] if b and b != [0]]
    for number in reversed(range(len(groups))):
        *slot_grads, d_query = backward_phase(
            f"backward_slots_{number}", queries, probs[number], groups[number], peaks[number],
            last_peaks, inverse, own=number == 0, grads=(grad, diag, d_query), last=number == 0,
        )
        if number == 0:
            own_grads, slot_grads = slot_grads[:2], slot_grads[2:]
        for place_in, bit in enumerate(bits_of[number]):
            back += [swap(x, "seq", 1 << bit) for x in slot_grads[2 * place_in : 2 * place_in + 2]]
    key_grad, value_grad = finish(core, spots, own_grads, back, total_parts)
    return normed, d_query, key_grad, value_grad


def solution(mesh):
    placed = (
        P("seq", "head"),
        P("seq", "head"),
        P("seq", "head"),
        P("seq"),
        P(),
        P("head"),
        P("seq", "head"),
    )
    return jax.shard_map(
        per_device,
        mesh=mesh,
        in_specs=placed,
        out_specs=(P("seq", "head"), P("seq", "head"), P("seq", "head"), P("seq", "head")),
        check_vma=False,
    )
```

```python
import functools
import math

import jax
import jax.numpy as jnp
from jax import lax
from jax.experimental import pallas as pl
from jax.experimental.pallas import tpu as pltpu
from jax.sharding import PartitionSpec as P

QH = 64
KVH = 8
HD = 128
GROUP = QH // KVH

NEG_FILL = -1e30
NORM_EPS = 1e-06
HIDDEN = 256.0
HIDDEN_ABOVE = 100.0
SCALING = HD ** (-0.5)
EXPONENT = SCALING * math.log2(math.e)
VMEM_BYTES = 56 * 2**20
TOTAL_LEAST = 2.0**-80
TOTAL_MOST = 2.0**100

F32 = jnp.float32
BF16 = jnp.bfloat16


def dot_nt(left, right):
    return lax.dot_general(left, right, (((1,), (1,)), ((), ())), preferred_element_type=F32)


def dot_nn(left, right):
    return lax.dot_general(left, right, (((1,), (0,)), ((), ())), preferred_element_type=F32)


def dot_tn(left, right):
    return lax.dot_general(left, right, (((0,), (0,)), ((), ())), preferred_element_type=F32)


def swap(block, axis, mask):
    count = lax.axis_size(axis)
    return lax.ppermute(block, axis, [(i, i ^ mask) for i in range(count)])


def params():
    return pltpu.CompilerParams(vmem_limit_bytes=VMEM_BYTES)


def cost(flops, moved, expos=0):
    return pl.CostEstimate(flops=int(flops), bytes_accessed=int(moved), transcendentals=int(expos))


def lane_of(shape):
    return lax.broadcasted_iota(jnp.int32, shape, 1)


def column_block(rows, width, row=0):
    return pl.BlockSpec((rows, width), lambda a: (row, a))


def fixed_block(shape):
    return pl.BlockSpec(shape, lambda a: (0,) * len(shape))


SCALAR = pl.BlockSpec(memory_space=pltpu.SMEM)
WHOLE = pl.BlockSpec(memory_space=pltpu.VMEM)


def read_global(refs, core_ref):
    count = len(refs) // 2
    mine = jnp.concatenate([r[...] for r in refs[:count]], 0)
    other = jnp.concatenate([r[...] for r in refs[count:]], 0)
    first = core_ref[0] == 0
    return jnp.where(first, mine, other), jnp.where(first, other, mine)


def read_slots(take, near, parts):
    keys, values = [], []
    for _ in range(near):
        keys.append(take(0)[...])
        values.append(take(0)[...])
    core_ref = None
    if parts:
        core_ref = take(0)
        refs = [take(0) for _ in range(parts)]
        k, v = read_global(refs, core_ref)
        keys.append(k)
        values.append(v)
    return keys, values, core_ref


def slot_operands(near, parts, core):
    args, specs = [], []
    for k, v, row in near:
        rows = k.shape[0] if row == 0 else k.shape[0] // 2
        args += [k, v]
        specs += [column_block(rows, HD), column_block(rows, HD, row)]
    if parts:
        args += [core] + list(parts)
        specs += [SCALAR] + [column_block(x.shape[0], HD) for x in parts]
    slots = sum(k.shape[0] if row == 0 else k.shape[0] // 2 for k, _, row in near)
    return args, specs, slots + sum(x.shape[0] for x in parts) // 2


def prepare_kernel(keep_ref, k_ref, v_ref, out_ref):
    rows, width = k_ref.shape
    keep = jnp.broadcast_to(keep_ref[...].astype(F32), (HD, rows)).T
    for start in range(0, width, HD):
        here = slice(start, start + HD)
        k = jnp.where(keep == 1.0, k_ref[:, here].astype(F32), HIDDEN)
        out_ref[:rows, here] = k.astype(BF16)
    out_ref[rows:, :] = v_ref[...]


def prepare(keep_row, keys, values):
    rows, width = keys.shape
    return pl.pallas_call(
        prepare_kernel,
        in_specs=[WHOLE] * 3,
        out_specs=WHOLE,
        out_shape=jax.ShapeDtypeStruct((2 * rows, width), BF16),
        compiler_params=params(),
        cost_estimate=cost(2**20, 4 * rows * width * 2),
        name="prepare_keys_values",
    )(keep_row, keys, values)


def forward_kernel(near, parts, own, first, last, *refs):
    refs = list(refs)
    take = refs.pop
    q_ref = take(0)
    key_list, value_list, _ = read_slots(take, near, parts)
    keep_ref = take(0) if own else None
    if not first:
        sum_ref, peak_ref, total_ref = take(0), take(0), take(0)
    if last:
        cot_ref, gain_ref = take(0), take(0)
    p_ref, out_ref, peak_out, total_out = take(0), take(0), take(0), take(0)
    if last:
        rows_ref, square_acc, cross_acc = take(0), take(0), take(0)
        step = pl.program_id(0)

    rows = q_ref.shape[0]
    lanes = lane_of((rows, HD))
    unit = (lanes == 0).astype(BF16)
    wide_keys, wide_values = [], []
    for number, (k, v) in enumerate(zip(key_list, value_list)):
        if own and number == 0:
            extra = jnp.zeros_like(k)
        else:
            hidden = (lane_of(k.shape) == 0) & (k.astype(F32) > HIDDEN_ABOVE)
            extra = jnp.where(hidden, NEG_FILL, 0.0).astype(BF16)
        wide_keys.append(jnp.concatenate([k, extra], 1))
        wide_values.append(jnp.concatenate([v, jnp.ones_like(v)], 1))
    if own:
        square = (rows, rows)
        itself = lax.broadcasted_iota(jnp.int32, square, 0) == lane_of(square)
        visible = itself | (jnp.broadcast_to(keep_ref[...], square) == 1)

    def scores_of(head, number):
        q = jnp.concatenate([q_ref[:, head * HD : (head + 1) * HD], unit], 1)
        return dot_nt(q, wide_keys[number])

    def keep_exponentials(head, number, value):
        start = sum(k.shape[0] for k in wide_keys[:number])
        stop = start + wide_keys[number].shape[0]
        p_ref[head * rows : (head + 1) * rows, start:stop] = value
        return dot_nn(value, wide_values[number])

    totals = jnp.ones((rows, HD), F32)
    order = [(head, number) for head in range(GROUP) for number in range(len(wide_keys))]
    ahead = scores_of(*order[0])
    mixed = None
    for place, (head, number) in enumerate(order):
        scores = ahead
        if place + 1 < len(order):
            ahead = scores_of(*order[place + 1])
        expo = jnp.exp2(scores * EXPONENT)
        if own and number == 0:
            expo = jnp.where(visible, expo, 0.0)
        part = keep_exponentials(head, number, expo.astype(BF16))
        mixed = part if number == 0 else mixed + part
        if number + 1 == len(wide_keys):
            here = slice(head * HD, (head + 1) * HD)
            value_sum, total = mixed[:, :HD], mixed[:, HD:]
            if not first:
                value_sum = value_sum + sum_ref[:, here]
                total = total + total_ref[:, head : head + 1]
            if last:
                total = 1.0 / total
                value_sum = value_sum * total
            out_ref[:, here] = value_sum
            totals = jnp.where(lanes == head, total, totals)
    total_out[...] = totals
    peak_out[...] = jnp.zeros((rows, HD), F32)
    if last:
        good = (totals >= 1.0 / TOTAL_MOST) & (totals <= 1.0 / TOTAL_LEAST)
    else:
        good = (totals >= TOTAL_LEAST) & (totals <= TOTAL_MOST)
    if not first:
        good = good & (peak_ref[...] == 0.0)
    in_range = jnp.min(jnp.where(good, 1.0, 0.0)) > 0.5

    @pl.when(jnp.logical_not(in_range))
    def _():
        peaks = jnp.zeros((rows, HD), F32)
        safe_totals = jnp.ones((rows, HD), F32)
        for head in range(GROUP):
            scores = [scores_of(head, number) for number in range(len(wide_keys))]
            if own:
                scores[0] = jnp.where(visible, scores[0], NEG_FILL)
            peak = functools.reduce(jnp.maximum, [jnp.max(s, -1, keepdims=True) for s in scores])
            if not first:
                before = peak_ref[:, head : head + 1]
                peak = jnp.maximum(peak, before)
            mix = None
            for number, s in enumerate(scores):
                e = jnp.exp2((s - peak) * EXPONENT).astype(BF16)
                part = keep_exponentials(head, number, e)
                mix = part if mix is None else mix + part
            here = slice(head * HD, (head + 1) * HD)
            value_sum, total = mix[:, :HD], mix[:, HD:]
            if not first:
                shrink = jnp.exp2((before - peak) * EXPONENT)
                value_sum = value_sum + sum_ref[:, here] * shrink
                total = total + total_ref[:, head : head + 1] * shrink
            if last:
                total = 1.0 / total
                value_sum = value_sum * total
            out_ref[:, here] = value_sum
            safe_totals = jnp.where(lanes == head, total, safe_totals)
            peaks = jnp.where(lanes == head, peak, peaks)
        peak_out[...] = peaks
        total_out[...] = safe_totals

    if last:

        @pl.when(step == 0)
        def _():
            square_acc[...] = jnp.zeros_like(square_acc)
            cross_acc[...] = jnp.zeros_like(cross_acc)

        squares, crosses = square_acc[...], cross_acc[...]
        for head in range(GROUP):
            here = slice(head * HD, (head + 1) * HD)
            attn = out_ref[:, here]
            upstream = cot_ref[:, here].astype(F32) * gain_ref[:, here].astype(F32)
            squares = squares + attn * attn
            crosses = crosses + upstream * attn
        square_acc[...] = squares
        cross_acc[...] = crosses

        @pl.when(step == pl.num_programs(0) - 1)
        def _():
            square_row = jnp.sum(square_acc[...].T, 0, keepdims=True)
            cross_row = jnp.sum(cross_acc[...].T, 0, keepdims=True)
            rows_ref[...] = jnp.concatenate([square_row, cross_row], 0)


def forward_phase(name, queries, near, parts=(), core=None, keep_row=None, before=None, norm=None):
    rows, width = queries.shape
    steps = width // (GROUP * HD)
    wide = GROUP * HD
    args, specs, slots = slot_operands(near, parts, core)
    args.insert(0, queries)
    specs.insert(0, column_block(rows, wide))
    if keep_row is not None:
        args.append(keep_row)
        specs.append(fixed_block(keep_row.shape))
    if before is not None:
        args += list(before)
        specs += [column_block(rows, wide), column_block(rows, HD), column_block(rows, HD)]
    if norm is not None:
        args += list(norm)
        specs += [column_block(rows, wide), column_block(1, wide)]
    out_shapes = [
        jax.ShapeDtypeStruct((steps * GROUP * rows, slots), BF16),
        jax.ShapeDtypeStruct((rows, width), F32),
        jax.ShapeDtypeStruct((rows, steps * HD), F32),
        jax.ShapeDtypeStruct((rows, steps * HD), F32),
    ]
    out_specs = [
        pl.BlockSpec((GROUP * rows, slots), lambda a: (a, 0)),
        column_block(rows, wide),
        column_block(rows, HD),
        column_block(rows, HD),
    ]
    scratch = []
    if norm is not None:
        out_shapes.append(jax.ShapeDtypeStruct((2, rows), F32))
        out_specs.append(fixed_block((2, rows)))
        scratch = [pltpu.VMEM((rows, HD), F32), pltpu.VMEM((rows, HD), F32)]
    elements = rows * slots * steps * GROUP
    return pl.pallas_call(
        functools.partial(
            forward_kernel, len(near), len(parts), keep_row is not None, before is None, norm is not None
        ),
        grid=(steps,),
        in_specs=specs,
        out_specs=out_specs,
        out_shape=out_shapes,
        scratch_shapes=scratch,
        compiler_params=params(),
        cost_estimate=cost(8 * elements * HD, 2 * elements, elements),
        name=name,
    )(*args)


def backward_kernel(near, parts, own, later, last, features, *refs):
    refs = list(refs)
    take = refs.pop
    first = later is not None
    q_ref, p_ref = take(0), take(0)
    key_list, value_list, core_ref = read_slots(take, near, parts)
    if first:
        peak_refs = [take(0) for _ in range(later + 1)]
        inverse_ref, norm_ref, attn_ref, cot_ref, gain_ref = [take(0) for _ in range(5)]
    else:
        grad_ref, diag_ref, dq_ref = take(0), take(0), take(0)
    outs = [take(0) for _ in range(near + parts)]
    dq_out = take(0)
    if first:
        normed_out = take(0)
        later_outs = [(take(0), take(0)) for _ in range(later)]
    ds_ref, q_stack, grad_stack = take(0), take(0), take(0)

    rows = q_ref.shape[0]
    lanes = lane_of((rows, HD))
    if first:
        inverse_total = inverse_ref[...]
        factors = [inverse_total] + [
            jnp.exp2((r[...] - peak_refs[0][...]) * EXPONENT) * inverse_total for r in peak_refs[1:]
        ]
        squares = norm_ref[0:1, :]
        crossed = norm_ref[1:2, :]
        inverse_row = lax.rsqrt(squares / features + NORM_EPS)
        coefficient_row = inverse_row * inverse_row * inverse_row * crossed / features
        inverse_wide = jnp.broadcast_to(inverse_row, (HD, rows)).T
        coefficient_wide = jnp.broadcast_to(coefficient_row, (HD, rows)).T
        diags = [jnp.zeros((rows, HD), F32)] * later

    gradients, diagonals = [], []
    for head in range(GROUP):
        here = slice(head * HD, (head + 1) * HD)
        stack = slice(head * rows, (head + 1) * rows)
        if first:
            attn = attn_ref[:, here]
            gain = gain_ref[:, here].astype(F32)
            normed_out[:, here] = (attn * inverse_wide * gain).astype(BF16)
            upstream = cot_ref[:, here].astype(F32) * gain
            grad = inverse_wide * upstream - attn * coefficient_wide
            diag = jnp.sum(grad * attn, -1, keepdims=True)
            factor = factors[0][:, head : head + 1]
            grad_bf = (grad * factor).astype(BF16)
            scaled_diag = diag * factor
            for number, (grad_out, _) in enumerate(later_outs):
                factor = factors[number + 1][:, head : head + 1]
                grad_out[:, here] = (grad * factor).astype(BF16)
                diags[number] = jnp.where(lanes == head, diag * factor, diags[number])
        else:
            grad_bf = grad_ref[:, here]
            scaled_diag = diag_ref[:, head : head + 1]
        grad_stack[stack, :] = grad_bf
        q_stack[stack, :] = q_ref[:, here]
        start = 0
        d_query = None
        for k, v in zip(key_list, value_list):
            columns = slice(start, start + k.shape[0])
            d_probs = dot_nt(grad_bf, v)
            d_scores = (p_ref[stack, columns].astype(F32) * (d_probs - scaled_diag)).astype(BF16)
            ds_ref[stack, columns] = d_scores
            part = dot_nn(d_scores, k)
            d_query = part if d_query is None else d_query + part
            start += k.shape[0]
        if not first:
            d_query = d_query + dq_ref[:, here]
        if last:
            d_query = d_query * SCALING
        dq_out[:, here] = d_query.astype(dq_out.dtype)
    if first:
        for (_, diag_out), diag in zip(later_outs, diags):
            diag_out[...] = diag
    q_all, grad_all = q_stack[...], grad_stack[...]
    start = 0
    for number, k in enumerate(key_list):
        size = k.shape[0]
        columns = slice(start, start + size)
        start += size
        d_key = (dot_tn(q_all, ds_ref[:, columns]) * SCALING).T
        d_value = dot_tn(grad_all, p_ref[:, columns]).T
        if number < near:
            out = outs[number]
            out[:size, :] = d_key.astype(out.dtype)
            out[size:, :] = d_value.astype(out.dtype)
        else:
            d_key, d_value = d_key.astype(BF16), d_value.astype(BF16)
            core_first = core_ref[0] == 0
            mine = jnp.where(core_first, d_key, d_value)
            other = jnp.where(core_first, d_value, d_key)
            begin = 0
            for part in range(parts // 2):
                mine_out, other_out = outs[near + part], outs[near + parts // 2 + part]
                length = mine_out.shape[0]
                mine_out[...] = mine[begin : begin + length]
                other_out[...] = other[begin : begin + length]
                begin += length


def backward_phase(
    name, queries, probs, near, parts=(), core=None, own=False, peaks=None, norm=None,
    grads=None, last=False,
):
    rows, width = queries.shape
    steps = width // (GROUP * HD)
    wide = GROUP * HD
    slots = probs.shape[1]
    args, specs, _ = slot_operands(near, parts, core)
    args = [queries, probs] + args
    specs = [column_block(rows, wide), pl.BlockSpec((GROUP * rows, slots), lambda a: (a, 0))] + specs
    out_shapes, out_specs = [], []
    for number, (k, _, row) in enumerate(near):
        size = k.shape[0] if row == 0 else k.shape[0] // 2
        kind = F32 if own and number == 0 else BF16
        out_shapes.append(jax.ShapeDtypeStruct((2 * size, k.shape[1]), kind))
        out_specs.append(column_block(2 * size, HD))
    for x in parts:
        out_shapes.append(jax.ShapeDtypeStruct(x.shape, BF16))
        out_specs.append(column_block(x.shape[0], HD))
    later = None
    if norm is not None:
        later = len(peaks) - 1
        inverse, sums, attn, cotangent, gain = norm
        args += list(peaks) + [inverse, sums, attn, cotangent, gain]
        specs += [column_block(rows, HD)] * (len(peaks) + 1) + [
            fixed_block(sums.shape),
            column_block(rows, wide),
            column_block(rows, wide),
            column_block(1, wide),
        ]
    else:
        args += list(grads)
        specs += [column_block(rows, wide), column_block(rows, HD), column_block(rows, wide)]
    out_shapes.append(jax.ShapeDtypeStruct((rows, width), BF16 if last else F32))
    out_specs.append(column_block(rows, wide))
    if norm is not None:
        out_shapes.append(jax.ShapeDtypeStruct((rows, width), BF16))
        out_specs.append(column_block(rows, wide))
        for _ in range(later):
            out_shapes += [
                jax.ShapeDtypeStruct((rows, width), BF16),
                jax.ShapeDtypeStruct((rows, steps * HD), F32),
            ]
            out_specs += [column_block(rows, wide), column_block(rows, HD)]
    elements = rows * slots * steps * GROUP
    return pl.pallas_call(
        functools.partial(backward_kernel, len(near), len(parts), own, later, last, QH * HD),
        grid=(steps,),
        in_specs=specs,
        out_specs=out_specs,
        out_shape=out_shapes,
        scratch_shapes=[
            pltpu.VMEM((GROUP * rows, slots), BF16),
            pltpu.VMEM((GROUP * rows, HD), BF16),
            pltpu.VMEM((GROUP * rows, HD), BF16),
        ],
        compiler_params=params(),
        cost_estimate=cost(12 * elements * HD, 2 * elements),
        name=name,
    )(*args)


def pick_kernel(core_ref, spots_ref, own_ref, partner_ref, out_ref):
    rows = own_ref.shape[0] // 2
    count = spots_ref.shape[1]
    first = core_ref[0] == 0
    row_ids = lax.broadcasted_iota(jnp.int32, (rows, count), 0)
    total = None
    for number, ref in enumerate((own_ref, partner_ref)):
        source = jnp.where(first, ref[:rows, :], ref[rows:, :])
        chosen = jnp.where(row_ids == spots_ref[number : number + 1, :], 1.0, 0.0).astype(BF16)
        part = dot_tn(chosen, source)
        total = part if total is None else total + part
    out_ref[...] = total.astype(BF16)


def pick(core, spots, own, partner):
    shape = (spots.shape[1], own.shape[1])
    return pl.pallas_call(
        pick_kernel,
        in_specs=[SCALAR] + [WHOLE] * 3,
        out_specs=WHOLE,
        out_shape=jax.ShapeDtypeStruct(shape, BF16),
        compiler_params=params(),
        cost_estimate=cost(2 * shape[0] * shape[1] * own.shape[0], 3 * 2**20),
        name="pick_globals",
    )(core, spots, own, partner)


def finish_kernel(partners, parts, *refs):
    core_ref, spots_ref, own = refs[:3]
    back = refs[3 : 3 + partners]
    total = refs[3 + partners : 3 + partners + parts]
    outs = refs[3 + partners + parts :]
    rows = own.shape[0] // 2
    count = spots_ref.shape[1]
    row_ids = lax.broadcasted_iota(jnp.int32, (rows, count), 0)
    chosen = jnp.where(row_ids == spots_ref[0:1, :], 1.0, 0.0).astype(BF16)
    global_grads = read_global(total, core_ref)
    for kind in range(2):
        here = slice(kind * rows, (kind + 1) * rows)
        running = own[here, :]
        for ref in back:
            running = running + ref[here, :].astype(F32)
        running = running + dot_nn(chosen, global_grads[kind])
        outs[kind][...] = running.astype(BF16)


def finish(core, spots, own, back, total):
    args = [own] + list(back) + list(total)
    rows, width = own.shape
    return pl.pallas_call(
        functools.partial(finish_kernel, len(back), len(total)),
        in_specs=[SCALAR] + [WHOLE] * (len(args) + 1),
        out_specs=[WHOLE] * 2,
        out_shape=[jax.ShapeDtypeStruct((rows // 2, width), BF16)] * 2,
        compiler_params=params(),
        cost_estimate=cost(2**28, 4 * 2**20),
        name="finish_key_value_grads",
    )(core, spots, *args)


def levels_of(bit_count):
    bits = list(range(1, bit_count))
    levels = []
    while bits:
        levels.insert(0, bits[-2:])
        bits = bits[:-2]
    return levels


def masks_of(level):
    return [
        sum(1 << bit for place, bit in enumerate(level) if number >> place & 1)
        for number in range(1 << len(level))
    ]


def reduce_level(block, masks):
    size = block.shape[0] // len(masks)
    running = block[:size].astype(F32)
    for number, mask in enumerate(masks):
        if number:
            moved = swap(block[number * size : (number + 1) * size], "seq", mask)
            running = running + moved.astype(F32)
    return running.astype(BF16)


def gather_level(block, masks):
    return [block if mask == 0 else swap(block, "seq", mask) for mask in masks]


def gather_parts(block, levels):
    mine = [block]
    for masks in reversed(levels):
        block = mine[0] if len(mine) == 1 else jnp.concatenate(mine, 0)
        mine = gather_level(block, masks)
    return mine + [swap(part, "seq", 1) for part in mine]


def reduce_parts(blocks, masks):
    running = blocks[0].astype(F32)
    for part, mask in zip(blocks[1:], masks[1:]):
        running = running + swap(part, "seq", mask).astype(F32)
    return running.astype(BF16)


def per_device(queries, keys, values, key_keep, global_positions, gain, cotangent):
    rows = queries.shape[0]
    bit_count = lax.axis_size("seq").bit_length() - 1
    place = lax.axis_index("seq")
    core = (place & 1).reshape(1)
    global_count = global_positions.shape[0]
    keep_row = key_keep.reshape(1, rows)
    gain_row = gain.reshape(1, -1)

    packed = prepare(keep_row, keys, values)
    near = [swap(packed, "seq", 1 << bit) for bit in range(bit_count)]

    levels = [masks_of(level) for level in levels_of(bit_count)]
    order = [0]
    for masks in levels:
        order = [base ^ mask for base in order for mask in masks]
    pieces = len(order)
    chunk_ids = (place >> 1) ^ jnp.array([mask >> 1 for mask in order], jnp.int32)
    chunks = global_positions.reshape(pieces, global_count // pieces)
    match = chunk_ids[:, None] == jnp.arange(pieces, dtype=jnp.int32)[None, :]
    ordered = jnp.sum(jnp.where(match[:, :, None], chunks[None], 0), 1).reshape(global_count)
    spots = jnp.stack([ordered - place * rows, ordered - (place ^ 1) * rows])

    picked = pick(core, spots, packed, near[0])
    for masks in levels:
        picked = reduce_level(picked, masks)
    global_parts = gather_parts(picked, levels)

    group_a = [(keys, values, 0)] + [(x, x, 1) for x in near[:-1]]
    group_b = [(x, x, 1) for x in near[-1:]]
    p_a, *state = forward_phase("forward_a", queries, group_a, keep_row=keep_row)
    peak_a = state[1]
    p_b, attn, peak_b, inverse, sums = forward_phase(
        "forward_b", queries, group_b, global_parts, core, before=state, norm=(cotangent, gain_row)
    )
    head_bits = lax.axis_size("head").bit_length() - 1
    for bit in range(head_bits):
        sums = sums + swap(sums, "head", 1 << bit)

    back_b, *rest = backward_phase(
        "backward_b", queries, p_b, group_b, global_parts, core, peaks=[peak_b, peak_a],
        norm=(inverse, sums, attn, cotangent, gain_row),
    )
    part_count = len(global_parts)
    global_grads, (d_query, normed, grad_a, diag_a) = rest[:part_count], rest[part_count:]
    half = part_count // 2
    reduced = [
        (a.astype(F32) + swap(b, "seq", 1).astype(F32)).astype(BF16)
        for a, b in zip(global_grads[:half], global_grads[half:])
    ]
    total = reduce_parts(reduced, levels[0]) if levels else reduced[0]
    for masks in levels[1:]:
        total = reduce_level(total, masks)
    total_parts = gather_parts(total, levels)

    own, *back_a, d_query = backward_phase(
        "backward_a", queries, p_a, group_a, own=True, grads=(grad_a, diag_a, d_query), last=True
    )
    back = [swap(x, "seq", 1 << bit) for bit, x in enumerate(back_a + [back_b])]
    key_grad, value_grad = finish(core, spots, own, back, total_parts)
    return normed, d_query, key_grad, value_grad


def solution(mesh):
    placed = (
        P("seq", "head"),
        P("seq", "head"),
        P("seq", "head"),
        P("seq"),
        P(),
        P("head"),
        P("seq", "head"),
    )
    return jax.shard_map(
        per_device,
        mesh=mesh,
        in_specs=placed,
        out_specs=(P("seq", "head"), P("seq", "head"), P("seq", "head"), P("seq", "head")),
        check_vma=False,
    )
```

```python
import functools
import math

import jax
import jax.numpy as jnp
from jax import lax
from jax.experimental import pallas as pl
from jax.experimental.pallas import tpu as pltpu
from jax.sharding import PartitionSpec as P

QH = 64
KVH = 8
HD = 128
GROUP = QH // KVH

NEG_FILL = -1e30
NORM_EPS = 1e-06
HIDDEN = 256.0
HIDDEN_ABOVE = 100.0
SCALING = HD ** (-0.5)
EXPONENT = SCALING * math.log2(math.e)
VMEM_BYTES = 28 * 2**20
FAR_STAYS = False
GLOBALS_STAY = False
TOTAL_LEAST = 2.0**-80
TOTAL_MOST = 2.0**100

F32 = jnp.float32
BF16 = jnp.bfloat16


def dot_nt(left, right):
    return lax.dot_general(left, right, (((1,), (1,)), ((), ())), preferred_element_type=F32)


def dot_nn(left, right):
    return lax.dot_general(left, right, (((1,), (0,)), ((), ())), preferred_element_type=F32)


def dot_tn(left, right):
    return lax.dot_general(left, right, (((0,), (0,)), ((), ())), preferred_element_type=F32)


def swap(block, axis, mask):
    count = lax.axis_size(axis)
    return lax.ppermute(block, axis, [(i, i ^ mask) for i in range(count)])


def off_chip(block):
    return pltpu.with_memory_space_constraint(block, pltpu.HBM)


def params():
    return pltpu.CompilerParams(vmem_limit_bytes=VMEM_BYTES)


def cost(flops, moved, expos=0):
    return pl.CostEstimate(flops=int(flops), bytes_accessed=int(moved), transcendentals=int(expos))


def lane_of(shape):
    return lax.broadcasted_iota(jnp.int32, shape, 1)


def column_block(rows, width, row=0):
    return pl.BlockSpec((rows, width), lambda a: (row, a))


def fixed_block(shape):
    return pl.BlockSpec(shape, lambda a: (0,) * len(shape))


SCALAR = pl.BlockSpec(memory_space=pltpu.SMEM)
WHOLE = pl.BlockSpec(memory_space=pltpu.VMEM)
ANYWHERE = pl.BlockSpec(memory_space=pl.ANY)


def read_global(refs, core_ref):
    count = len(refs) // 2
    mine = jnp.concatenate([r[...] for r in refs[:count]], 0)
    other = jnp.concatenate([r[...] for r in refs[count:]], 0)
    first = core_ref[0] == 0
    return jnp.where(first, mine, other), jnp.where(first, other, mine)


def read_slots(take, near, parts):
    keys, values = [], []
    for _ in range(near):
        keys.append(take(0)[...])
        values.append(take(0)[...])
    core_ref = None
    if parts:
        core_ref = take(0)
        refs = [take(0) for _ in range(parts)]
        k, v = read_global(refs, core_ref)
        keys.append(k)
        values.append(v)
    return keys, values, core_ref


def slot_operands(near, parts, core):
    args, specs = [], []
    for k, v, row in near:
        rows = k.shape[0] if row == 0 else k.shape[0] // 2
        args += [k, v]
        specs += [column_block(rows, HD), column_block(rows, HD, row)]
    if parts:
        args += [core] + list(parts)
        specs += [SCALAR] + [column_block(x.shape[0], HD) for x in parts]
    slots = sum(k.shape[0] if row == 0 else k.shape[0] // 2 for k, _, row in near)
    return args, specs, slots + sum(x.shape[0] for x in parts) // 2


def prepare_kernel(keep_ref, k_ref, v_ref, out_ref):
    rows, width = k_ref.shape
    keep = jnp.broadcast_to(keep_ref[...].astype(F32), (HD, rows)).T
    for start in range(0, width, HD):
        here = slice(start, start + HD)
        k = jnp.where(keep == 1.0, k_ref[:, here].astype(F32), HIDDEN)
        out_ref[:rows, here] = k.astype(BF16)
    out_ref[rows:, :] = v_ref[...]


def prepare(keep_row, keys, values):
    rows, width = keys.shape
    return pl.pallas_call(
        prepare_kernel,
        in_specs=[WHOLE] * 3,
        out_specs=WHOLE,
        out_shape=jax.ShapeDtypeStruct((2 * rows, width), BF16),
        compiler_params=params(),
        cost_estimate=cost(2**20, 4 * rows * width * 2),
        name="prepare_keys_values",
    )(keep_row, keys, values)


def forward_kernel(near, parts, own, first, last, kept, resident, waits, *refs):
    refs = list(refs)
    take = refs.pop
    for _ in range(waits):
        take(0)
    q_ref = take(0)
    key_list, value_list, _ = read_slots(take, near, parts)
    keep_ref = take(0) if own else None
    if not first:
        sum_ref, peak_ref, total_ref = take(0), take(0), take(0)
    if last:
        cot_ref, gain_ref = take(0), take(0)
    p_refs = [take(0) for _ in kept]
    out_ref, peak_out, total_out = take(0), take(0), take(0)
    if last:
        rows_ref, square_acc, cross_acc = take(0), take(0), take(0)
        step = pl.program_id(0)

    rows = q_ref.shape[0]
    base = pl.multiple_of(pl.program_id(0) * (GROUP * rows), GROUP * rows)
    lanes = lane_of((rows, HD))
    unit = (lanes == 0).astype(BF16)
    wide_keys, wide_values = [], []
    for number, (k, v) in enumerate(zip(key_list, value_list)):
        if own and number == 0:
            extra = jnp.zeros_like(k)
        else:
            hidden = (lane_of(k.shape) == 0) & (k.astype(F32) > HIDDEN_ABOVE)
            extra = jnp.where(hidden, NEG_FILL, 0.0).astype(BF16)
        wide_keys.append(jnp.concatenate([k, extra], 1))
        wide_values.append(jnp.concatenate([v, jnp.ones_like(v)], 1))
    if own:
        square = (rows, rows)
        itself = lax.broadcasted_iota(jnp.int32, square, 0) == lane_of(square)
        visible = itself | (jnp.broadcast_to(keep_ref[...], square) == 1)

    def scores_of(head, number):
        q = jnp.concatenate([q_ref[:, head * HD : (head + 1) * HD], unit], 1)
        return dot_nt(q, wide_keys[number])

    def keep_exponentials(head, number, value):
        group = next(i for i, members in enumerate(kept) if number in members)
        start = sum(wide_keys[i].shape[0] for i in kept[group] if i < number)
        stop = start + wide_keys[number].shape[0]
        lower = base + head * rows if resident[group] else head * rows
        p_refs[group][pl.ds(lower, rows), start:stop] = value
        return dot_nn(value, wide_values[number])

    totals = jnp.ones((rows, HD), F32)
    order = [(head, number) for head in range(GROUP) for number in range(len(wide_keys))]
    ahead = scores_of(*order[0])
    mixed = None
    for place, (head, number) in enumerate(order):
        scores = ahead
        if place + 1 < len(order):
            ahead = scores_of(*order[place + 1])
        expo = jnp.exp2(scores * EXPONENT)
        if own and number == 0:
            expo = jnp.where(visible, expo, 0.0)
        part = keep_exponentials(head, number, expo.astype(BF16))
        mixed = part if number == 0 else mixed + part
        if number + 1 == len(wide_keys):
            here = slice(head * HD, (head + 1) * HD)
            value_sum, total = mixed[:, :HD], mixed[:, HD:]
            if not first:
                value_sum = value_sum + sum_ref[:, here]
                total = total + total_ref[:, head : head + 1]
            if last:
                total = 1.0 / total
                value_sum = value_sum * total
            out_ref[:, here] = value_sum
            totals = jnp.where(lanes == head, total, totals)
    total_out[...] = totals
    peak_out[...] = jnp.zeros((rows, HD), F32)
    if last:
        good = (totals >= 1.0 / TOTAL_MOST) & (totals <= 1.0 / TOTAL_LEAST)
    else:
        good = (totals >= TOTAL_LEAST) & (totals <= TOTAL_MOST)
    if not first:
        good = good & (peak_ref[...] == 0.0)
    in_range = jnp.min(jnp.where(good, 1.0, 0.0)) > 0.5

    @pl.when(jnp.logical_not(in_range))
    def _():
        peaks = jnp.zeros((rows, HD), F32)
        safe_totals = jnp.ones((rows, HD), F32)
        for head in range(GROUP):
            scores = [scores_of(head, number) for number in range(len(wide_keys))]
            if own:
                scores[0] = jnp.where(visible, scores[0], NEG_FILL)
            peak = functools.reduce(jnp.maximum, [jnp.max(s, -1, keepdims=True) for s in scores])
            if not first:
                before = peak_ref[:, head : head + 1]
                peak = jnp.maximum(peak, before)
            mix = None
            for number, s in enumerate(scores):
                e = jnp.exp2((s - peak) * EXPONENT).astype(BF16)
                part = keep_exponentials(head, number, e)
                mix = part if mix is None else mix + part
            here = slice(head * HD, (head + 1) * HD)
            value_sum, total = mix[:, :HD], mix[:, HD:]
            if not first:
                shrink = jnp.exp2((before - peak) * EXPONENT)
                value_sum = value_sum + sum_ref[:, here] * shrink
                total = total + total_ref[:, head : head + 1] * shrink
            if last:
                total = 1.0 / total
                value_sum = value_sum * total
            out_ref[:, here] = value_sum
            safe_totals = jnp.where(lanes == head, total, safe_totals)
            peaks = jnp.where(lanes == head, peak, peaks)
        peak_out[...] = peaks
        total_out[...] = safe_totals

    if last:

        @pl.when(step == 0)
        def _():
            square_acc[...] = jnp.zeros_like(square_acc)
            cross_acc[...] = jnp.zeros_like(cross_acc)

        squares, crosses = square_acc[...], cross_acc[...]
        for head in range(GROUP):
            here = slice(head * HD, (head + 1) * HD)
            attn = out_ref[:, here]
            upstream = cot_ref[:, here].astype(F32) * gain_ref[:, here].astype(F32)
            squares = squares + attn * attn
            crosses = crosses + upstream * attn
        square_acc[...] = squares
        cross_acc[...] = crosses

        @pl.when(step == pl.num_programs(0) - 1)
        def _():
            square_row = jnp.sum(square_acc[...].T, 0, keepdims=True)
            cross_row = jnp.sum(cross_acc[...].T, 0, keepdims=True)
            rows_ref[...] = jnp.concatenate([square_row, cross_row], 0)


def forward_phase(
    name, queries, near, parts=(), core=None, keep_row=None, before=None, norm=None, kept=None,
    resident=(False, False), after=(),
):
    rows, width = queries.shape
    steps = width // (GROUP * HD)
    wide = GROUP * HD
    args, specs, slots = slot_operands(near, parts, core)
    block_rows = [rows] * len(near) + ([slots - rows * len(near)] if parts else [])
    sizes = [slots] if kept is None else [sum(block_rows[i] for i in members) for members in kept]
    kept = [range(len(near) + 1)] if kept is None else kept
    args = list(after) + [queries] + args
    specs = [ANYWHERE] * len(after) + [column_block(rows, wide)] + specs
    if keep_row is not None:
        args.append(keep_row)
        specs.append(fixed_block(keep_row.shape))
    if before is not None:
        args += list(before)
        specs += [column_block(rows, wide), column_block(rows, HD), column_block(rows, HD)]
    if norm is not None:
        args += list(norm)
        specs += [column_block(rows, wide), column_block(1, wide)]
    place = jax.ShapeDtypeStruct if norm is None else pltpu.HBM
    out_shapes = [pltpu.HBM((steps * GROUP * rows, size), BF16) for size in sizes] + [
        place((rows, width), F32),
        jax.ShapeDtypeStruct((rows, steps * HD), F32),
        jax.ShapeDtypeStruct((rows, steps * HD), F32),
    ]
    out_specs = [
        WHOLE if stay else pl.BlockSpec((GROUP * rows, size), lambda a: (a, 0))
        for size, stay in zip(sizes, resident)
    ] + [
        column_block(rows, wide),
        column_block(rows, HD),
        column_block(rows, HD),
    ]
    scratch = []
    if norm is not None:
        out_shapes.append(jax.ShapeDtypeStruct((2, rows), F32))
        out_specs.append(fixed_block((2, rows)))
        scratch = [pltpu.VMEM((rows, HD), F32), pltpu.VMEM((rows, HD), F32)]
    elements = rows * slots * steps * GROUP
    return pl.pallas_call(
        functools.partial(
            forward_kernel, len(near), len(parts), keep_row is not None, before is None,
            norm is not None, kept, resident, len(after),
        ),
        grid=(steps,),
        in_specs=specs,
        out_specs=out_specs,
        out_shape=out_shapes,
        scratch_shapes=scratch,
        compiler_params=params(),
        cost_estimate=cost(8 * elements * HD, 2 * elements, elements),
        name=name,
    )(*args)


def backward_kernel(near, parts, own, later, last, features, added, resident, waits, *refs):
    refs = list(refs)
    take = refs.pop
    for _ in range(waits):
        take(0)
    first = later is not None
    q_ref, p_ref = take(0), take(0)
    key_list, value_list, core_ref = read_slots(take, near, parts)
    if first:
        peak_refs = [take(0) for _ in range(later + 1)]
        inverse_ref, norm_ref, other_ref, attn_ref, cot_ref, gain_ref = [take(0) for _ in range(6)]
    else:
        grad_ref, diag_ref, dq_ref = take(0), take(0), take(0)
    add_refs = [take(0) for _ in range(added)]
    outs = [take(0) for _ in range(near + parts)]
    dq_out = take(0)
    if first:
        normed_out = take(0)
        later_outs = [(take(0), take(0)) for _ in range(later)]
    ds_ref, q_stack, grad_stack = take(0), take(0), take(0)

    rows = q_ref.shape[0]
    base = 0
    if resident:
        base = pl.multiple_of(pl.program_id(0) * (GROUP * rows), GROUP * rows)
    lanes = lane_of((rows, HD))
    if first:
        inverse_total = inverse_ref[...]
        factors = [inverse_total] + [
            jnp.exp2((r[...] - peak_refs[0][...]) * EXPONENT) * inverse_total for r in peak_refs[1:]
        ]
        squares = norm_ref[0:1, :] + other_ref[0:1, :]
        crossed = norm_ref[1:2, :] + other_ref[1:2, :]
        inverse_row = lax.rsqrt(squares / features + NORM_EPS)
        coefficient_row = inverse_row * inverse_row * inverse_row * crossed / features
        inverse_wide = jnp.broadcast_to(inverse_row, (HD, rows)).T
        coefficient_wide = jnp.broadcast_to(coefficient_row, (HD, rows)).T
        diags = [jnp.zeros((rows, HD), F32)] * later

    gradients, diagonals = [], []
    for head in range(GROUP):
        here = slice(head * HD, (head + 1) * HD)
        stack = slice(head * rows, (head + 1) * rows)
        if first:
            attn = attn_ref[:, here]
            gain = gain_ref[:, here].astype(F32)
            normed_out[:, here] = (attn * inverse_wide * gain).astype(BF16)
            upstream = cot_ref[:, here].astype(F32) * gain
            grad = inverse_wide * upstream - attn * coefficient_wide
            diag = jnp.sum(grad * attn, -1, keepdims=True)
            factor = factors[0][:, head : head + 1]
            grad_bf = (grad * factor).astype(BF16)
            scaled_diag = diag * factor
            for number, (grad_out, _) in enumerate(later_outs):
                factor = factors[number + 1][:, head : head + 1]
                grad_out[:, here] = (grad * factor).astype(BF16)
                diags[number] = jnp.where(lanes == head, diag * factor, diags[number])
        else:
            grad_bf = grad_ref[:, here]
            scaled_diag = diag_ref[:, head : head + 1]
        grad_stack[stack, :] = grad_bf
        q_stack[stack, :] = q_ref[:, here]
        start = 0
        d_query = None
        for k, v in zip(key_list, value_list):
            columns = slice(start, start + k.shape[0])
            d_probs = dot_nt(grad_bf, v)
            d_scores = (p_ref[pl.ds(base + head * rows, rows), columns].astype(F32) * (d_probs - scaled_diag)).astype(BF16)
            ds_ref[stack, columns] = d_scores
            part = dot_nn(d_scores, k)
            d_query = part if d_query is None else d_query + part
            start += k.shape[0]
        if not first:
            d_query = d_query + dq_ref[:, here]
        if last:
            d_query = d_query * SCALING
        dq_out[:, here] = d_query.astype(dq_out.dtype)
    if first:
        for (_, diag_out), diag in zip(later_outs, diags):
            diag_out[...] = diag
    q_all, grad_all = q_stack[...], grad_stack[...]
    start = 0
    for number, k in enumerate(key_list):
        size = k.shape[0]
        columns = slice(start, start + size)
        start += size
        d_key = (dot_tn(q_all, ds_ref[:, columns]) * SCALING).T
        d_value = dot_tn(grad_all, p_ref[pl.ds(base, GROUP * rows), columns]).T
        if number < near:
            out = outs[number]
            if own and number == 0:
                for ref in add_refs:
                    d_key = d_key + ref[:size, :].astype(F32)
                    d_value = d_value + ref[size:, :].astype(F32)
            out[:size, :] = d_key.astype(out.dtype)
            out[size:, :] = d_value.astype(out.dtype)
        else:
            d_key, d_value = d_key.astype(BF16), d_value.astype(BF16)
            core_first = core_ref[0] == 0
            mine = jnp.where(core_first, d_key, d_value)
            other = jnp.where(core_first, d_value, d_key)
            begin = 0
            for part in range(parts // 2):
                mine_out, other_out = outs[near + part], outs[near + parts // 2 + part]
                length = mine_out.shape[0]
                mine_out[...] = mine[begin : begin + length]
                other_out[...] = other[begin : begin + length]
                begin += length


def backward_phase(
    name, queries, probs, near, parts=(), core=None, own=False, peaks=None, norm=None,
    grads=None, last=False, add=(), resident=False,
    after=(),
):
    rows, width = queries.shape
    steps = width // (GROUP * HD)
    wide = GROUP * HD
    slots = probs.shape[1]
    args, specs, _ = slot_operands(near, parts, core)
    args = list(after) + [queries, off_chip(probs)] + args
    specs = [ANYWHERE] * len(after) + [
        column_block(rows, wide),
        WHOLE if resident else pl.BlockSpec((GROUP * rows, slots), lambda a: (a, 0)),
    ] + specs
    out_shapes, out_specs = [], []
    for number, (k, _, row) in enumerate(near):
        size = k.shape[0] if row == 0 else k.shape[0] // 2
        kind = F32 if own and number == 0 else BF16
        out_shapes.append(jax.ShapeDtypeStruct((2 * size, k.shape[1]), kind))
        out_specs.append(column_block(2 * size, HD))
    for x in parts:
        out_shapes.append(jax.ShapeDtypeStruct(x.shape, BF16))
        out_specs.append(column_block(x.shape[0], HD))
    later = None
    if norm is not None:
        later = len(peaks) - 1
        inverse, sums, others, attn, cotangent, gain = norm
        args += list(peaks) + [inverse, sums, others, off_chip(attn), cotangent, gain]
        specs += [column_block(rows, HD)] * (len(peaks) + 1) + [
            fixed_block(sums.shape),
            fixed_block(others.shape),
            column_block(rows, wide),
            column_block(rows, wide),
            column_block(1, wide),
        ]
    else:
        args += list(grads)
        specs += [column_block(rows, wide), column_block(rows, HD), column_block(rows, wide)]
    args += list(add)
    specs += [column_block(x.shape[0], HD) for x in add]
    out_shapes.append(jax.ShapeDtypeStruct((rows, width), BF16 if last else F32))
    out_specs.append(column_block(rows, wide))
    if norm is not None:
        out_shapes.append(jax.ShapeDtypeStruct((rows, width), BF16))
        out_specs.append(column_block(rows, wide))
        for _ in range(later):
            out_shapes += [
                jax.ShapeDtypeStruct((rows, width), BF16),
                jax.ShapeDtypeStruct((rows, steps * HD), F32),
            ]
            out_specs += [column_block(rows, wide), column_block(rows, HD)]
    elements = rows * slots * steps * GROUP
    return pl.pallas_call(
        functools.partial(
            backward_kernel, len(near), len(parts), own, later, last, QH * HD, len(add), resident,
            len(after),
        ),
        grid=(steps,),
        in_specs=specs,
        out_specs=out_specs,
        out_shape=out_shapes,
        scratch_shapes=[
            pltpu.VMEM((GROUP * rows, slots), BF16),
            pltpu.VMEM((GROUP * rows, HD), BF16),
            pltpu.VMEM((GROUP * rows, HD), BF16),
        ],
        compiler_params=params(),
        cost_estimate=cost(12 * elements * HD, 2 * elements),
        name=name,
    )(*args)


def pick_kernel(core_ref, spots_ref, own_ref, partner_ref, *refs):
    out_refs = refs[2:]
    rows = own_ref.shape[0] // 2
    count = spots_ref.shape[1]
    first = core_ref[0] == 0
    row_ids = lax.broadcasted_iota(jnp.int32, (rows, count), 0)
    total = None
    for number, ref in enumerate((own_ref, partner_ref)):
        source = jnp.where(first, ref[:rows, :], ref[rows:, :])
        chosen = jnp.where(row_ids == spots_ref[number : number + 1, :], 1.0, 0.0).astype(BF16)
        part = dot_tn(chosen, source)
        total = part if total is None else total + part
    write_pieces(total, out_refs)


def write_pieces(total, out_refs):
    start = 0
    for ref in out_refs:
        ref[...] = total[start : start + ref.shape[0]].astype(ref.dtype)
        start += ref.shape[0]


def piece_shapes(count, rows, width):
    return [jax.ShapeDtypeStruct((rows // count, width), BF16)] * count


def pick(core, spots, own, partner, pieces):
    count, width = spots.shape[1], own.shape[1]
    return pl.pallas_call(
        pick_kernel,
        in_specs=[SCALAR] + [WHOLE] * 3 + [ANYWHERE],
        out_specs=[ANYWHERE] + [WHOLE] * pieces,
        out_shape=[jax.ShapeDtypeStruct(own.shape, own.dtype)] + piece_shapes(pieces, count, width),
        input_output_aliases={4: 0},
        compiler_params=params(),
        cost_estimate=cost(2 * count * width * own.shape[0], 3 * 2**20),
        name="pick_globals",
    )(core, spots, own, partner, own)


def combine_kernel(waits, blocks, *refs):
    blocks_in = refs[waits : waits + blocks]
    running = blocks_in[0][...].astype(F32)
    for ref in blocks_in[1:]:
        running = running + ref[...].astype(F32)
    write_pieces(running, refs[waits + blocks :])


def combine(blocks, pieces, after=()):
    rows, width = blocks[0].shape
    return pl.pallas_call(
        functools.partial(combine_kernel, len(after), len(blocks)),
        in_specs=[ANYWHERE] * len(after) + [WHOLE] * len(blocks),
        out_specs=[WHOLE] * pieces,
        out_shape=piece_shapes(pieces, rows, width),
        compiler_params=params(),
        cost_estimate=cost(2**20, len(blocks) * rows * width * 4),
        name="combine_globals",
    )(*after, *blocks)


def join_kernel(waits, blocks, *refs):
    out_ref = refs[-1]
    start = 0
    for ref in refs[waits : waits + blocks]:
        out_ref[start : start + ref.shape[0], :] = ref[...]
        start += ref.shape[0]


def join(blocks, after=()):
    rows = sum(x.shape[0] for x in blocks)
    width = blocks[0].shape[1]
    return pl.pallas_call(
        functools.partial(join_kernel, len(after), len(blocks)),
        in_specs=[ANYWHERE] * len(after) + [WHOLE] * len(blocks),
        out_specs=WHOLE,
        out_shape=jax.ShapeDtypeStruct((rows, width), BF16),
        compiler_params=params(),
        cost_estimate=cost(2**20, rows * width * 4),
        name="join_globals",
    )(*after, *blocks)


def settle_kernel(waits, *refs):
    own_ref, far_keys_ref, far_values_ref = refs[waits : waits + 3]
    refs = refs[waits + 3 : -3] + refs[-2:-1]
    rows = far_keys_ref.shape[0]
    for here, far_ref in ((slice(0, rows), far_keys_ref), (slice(rows, 2 * rows), far_values_ref)):
        running = own_ref[here, :] + far_ref[...].astype(F32)
        for ref in refs[:-1]:
            running = running + ref[here, :].astype(F32)
        refs[-1][here, :] = running


def settle(own, back, far_keys, far_values, through, after=()):
    return pl.pallas_call(
        functools.partial(settle_kernel, len(after)),
        in_specs=[ANYWHERE] * len(after) + [WHOLE] * (3 + len(back)) + [ANYWHERE],
        out_specs=[WHOLE, ANYWHERE],
        out_shape=[jax.ShapeDtypeStruct(x.shape, x.dtype) for x in (own, through)],
        input_output_aliases={len(after) + 3 + len(back): 1},
        compiler_params=params(),
        cost_estimate=cost(2**20, 4 * 2**20),
        name="settle_partner_grads",
    )(*after, own, far_keys, far_values, *back, through)


def finish_kernel(partners, parts, *refs):
    core_ref, spots_ref, own = refs[:3]
    back = refs[3 : 3 + partners]
    total = refs[3 + partners : 3 + partners + parts]
    outs = refs[3 + partners + parts :]
    rows = own.shape[0] // 2
    count = spots_ref.shape[1]
    row_ids = lax.broadcasted_iota(jnp.int32, (rows, count), 0)
    chosen = jnp.where(row_ids == spots_ref[0:1, :], 1.0, 0.0).astype(BF16)
    global_grads = read_global(total, core_ref)
    for kind in range(2):
        here = slice(kind * rows, (kind + 1) * rows)
        running = own[here, :]
        for ref in back:
            running = running + ref[here, :].astype(F32)
        running = running + dot_nn(chosen, global_grads[kind])
        outs[kind][...] = running.astype(BF16)


def finish(core, spots, own, back, total):
    args = [own] + list(back) + list(total)
    rows, width = own.shape
    return pl.pallas_call(
        functools.partial(finish_kernel, len(back), len(total)),
        in_specs=[SCALAR] + [WHOLE] * (len(args) + 1),
        out_specs=[WHOLE] * 2,
        out_shape=[jax.ShapeDtypeStruct((rows // 2, width), BF16)] * 2,
        compiler_params=params(),
        cost_estimate=cost(2**28, 4 * 2**20),
        name="finish_key_value_grads",
    )(core, spots, *args)


def levels_of(bit_count):
    bits = list(range(1, bit_count))
    levels = []
    while bits:
        levels.insert(0, bits[-2:])
        bits = bits[:-2]
    return levels


def masks_of(level):
    return [
        sum(1 << bit for place, bit in enumerate(level) if number >> place & 1)
        for number in range(1 << len(level))
    ]


def exchange(blocks, masks):
    return [blocks[0]] + [swap(x, "seq", mask) for x, mask in zip(blocks[1:], masks[1:])]


def spread(block, masks):
    return [block] + [swap(block, "seq", mask) for mask in masks[1:]]


def per_device(queries, keys, values, key_keep, global_positions, gain, cotangent):
    rows = queries.shape[0]
    bit_count = lax.axis_size("seq").bit_length() - 1
    place = lax.axis_index("seq")
    core = (place & 1).reshape(1)
    global_count = global_positions.shape[0]
    keep_row = key_keep.reshape(1, rows)
    gain_row = gain.reshape(1, -1)
    queries, cotangent = off_chip(queries), off_chip(cotangent)

    packed = prepare(keep_row, keys, values)
    near = [swap(packed, "seq", 1)]

    levels = [masks_of(level) for level in levels_of(bit_count)]
    order = [0]
    for masks in levels:
        order = [base ^ mask for base in order for mask in masks]
    pieces = len(order)
    chunk_ids = (place >> 1) ^ jnp.array([mask >> 1 for mask in order], jnp.int32)
    chunks = global_positions.reshape(pieces, global_count // pieces)
    match = chunk_ids[:, None] == jnp.arange(pieces, dtype=jnp.int32)[None, :]
    ordered = jnp.sum(jnp.where(match[:, :, None], chunks[None], 0), 1).reshape(global_count)
    spots = jnp.stack([ordered - place * rows, ordered - (place ^ 1) * rows])

    outer, inner = levels
    packed, *picked = pick(core, spots, packed, near[0], len(outer))
    moved = exchange(picked, outer)
    near += [swap(packed, "seq", 1 << bit) for bit in range(1, bit_count)]

    group_1 = [(off_chip(keys), off_chip(values), 0), (near[0], near[0], 1)]
    group_2 = [(x, x, 1) for x in near[1:-1]]
    group_3 = [(near[-1], near[-1], 1)]

    p_1, *state_1 = forward_phase("forward_own", queries, group_1, keep_row=keep_row, after=picked[-1:])
    summed = combine(moved, len(inner), after=state_1[2:])
    moved = exchange(summed, inner)
    p_2, *state_2 = forward_phase(
        "forward_partners", queries, group_2, before=state_1, after=summed[-1:]
    )
    (piece,) = combine(moved, 1, after=state_2[2:])
    half = join(spread(piece, inner))
    mine = spread(half, outer)
    global_parts = mine + [swap(part, "seq", 1) for part in mine]
    p_3, attn, peak_3, inverse, sums = forward_phase(
        "forward_globals", queries, group_3, global_parts, core, before=state_2,
        norm=(cotangent, gain_row),
    )
    head_bits = lax.axis_size("head").bit_length() - 1
    others = jnp.zeros_like(sums)
    for bit in range(head_bits):
        sums = sums + others if bit else sums
        others = swap(sums, "head", 1 << bit)

    count = len(global_parts)
    back_3, *rest = backward_phase(
        "backward_globals", queries, p_3, group_3, global_parts, core,
        peaks=[peak_3, state_2[1], state_1[1]], norm=(inverse, sums, others, attn, cotangent, gain_row),
    )
    global_grads, (d_query, normed, grad_2, diag_2, grad_1, diag_1) = rest[:count], rest[count:]
    kept, given = global_grads[: count // 2], global_grads[count // 2 :]
    reduced = [combine([a, swap(b, "seq", 1)], 1)[0] for a, b in zip(kept, given)]
    summed = combine(exchange(reduced, outer), len(inner))
    moved = exchange(summed, inner)
    far_mask = 1 << (bit_count - 1)
    far_keys = swap(back_3[:rows], "seq", far_mask)
    *back_2, d_query = backward_phase(
        "backward_partners", queries, p_2, group_2, grads=(grad_2, diag_2, d_query), after=summed[-1:]
    )
    (piece,) = combine(moved, 1, after=[d_query])
    moved = spread(piece, inner)
    half = join(moved)
    mine = spread(half, outer)
    far_values = swap(back_3[rows:], "seq", far_mask)
    own, back_first, d_query = backward_phase(
        "backward_own", queries, p_1, group_1, own=True, grads=(grad_1, diag_1, d_query), last=True,
        after=[half, far_keys],
    )
    back_2 = [swap(x, "seq", 2 << number) for number, x in enumerate(back_2)]
    own, back_first = settle(own, back_2, far_keys, far_values, back_first, after=mine[1:])
    total_parts = mine + [swap(part, "seq", 1) for part in mine]
    key_grad, value_grad = finish(core, spots, own, [swap(back_first, "seq", 1)], total_parts)
    return normed, d_query, key_grad, value_grad


def solution(mesh):
    placed = (
        P("seq", "head"),
        P("seq", "head"),
        P("seq", "head"),
        P("seq"),
        P(),
        P("head"),
        P("seq", "head"),
    )
    return jax.shard_map(
        per_device,
        mesh=mesh,
        in_specs=placed,
        out_specs=(P("seq", "head"), P("seq", "head"), P("seq", "head"), P("seq", "head")),
        check_vma=False,
    )
```

```python
import functools
import math

import jax
import jax.numpy as jnp
from jax import lax
from jax.experimental import pallas as pl
from jax.experimental.pallas import tpu as pltpu
from jax.sharding import PartitionSpec as P

QH = 64
KVH = 8
HD = 128
GROUP = QH // KVH

NEG_FILL = -1e30
NORM_EPS = 1e-06
HIDDEN = 256.0
HIDDEN_ABOVE = 100.0
SCALING = HD ** (-0.5)
EXPONENT = SCALING * math.log2(math.e)
VMEM_BYTES = 28 * 2**20
FAR_STAYS = False
GLOBALS_STAY = False
TOTAL_LEAST = 2.0**-80
TOTAL_MOST = 2.0**100

F32 = jnp.float32
BF16 = jnp.bfloat16


def dot_nt(left, right):
    return lax.dot_general(left, right, (((1,), (1,)), ((), ())), preferred_element_type=F32)


def dot_nn(left, right):
    return lax.dot_general(left, right, (((1,), (0,)), ((), ())), preferred_element_type=F32)


def dot_tn(left, right):
    return lax.dot_general(left, right, (((0,), (0,)), ((), ())), preferred_element_type=F32)


def swap(block, axis, mask):
    count = lax.axis_size(axis)
    return lax.ppermute(block, axis, [(i, i ^ mask) for i in range(count)])


def off_chip(block):
    return pltpu.with_memory_space_constraint(block, pltpu.HBM)


def params():
    return pltpu.CompilerParams(vmem_limit_bytes=VMEM_BYTES)


def cost(flops, moved, expos=0):
    return pl.CostEstimate(flops=int(flops), bytes_accessed=int(moved), transcendentals=int(expos))


def lane_of(shape):
    return lax.broadcasted_iota(jnp.int32, shape, 1)


def column_block(rows, width, row=0):
    return pl.BlockSpec((rows, width), lambda a: (row, a))


def fixed_block(shape):
    return pl.BlockSpec(shape, lambda a: (0,) * len(shape))


SCALAR = pl.BlockSpec(memory_space=pltpu.SMEM)
WHOLE = pl.BlockSpec(memory_space=pltpu.VMEM)
ANYWHERE = pl.BlockSpec(memory_space=pl.ANY)


def read_global(refs, core_ref):
    count = len(refs) // 2
    mine = jnp.concatenate([r[...] for r in refs[:count]], 0)
    other = jnp.concatenate([r[...] for r in refs[count:]], 0)
    first = core_ref[0] == 0
    return jnp.where(first, mine, other), jnp.where(first, other, mine)


def read_slots(take, near, parts):
    keys, values = [], []
    for _ in range(near):
        keys.append(take(0)[...])
        values.append(take(0)[...])
    core_ref = None
    if parts:
        core_ref = take(0)
        refs = [take(0) for _ in range(parts)]
        k, v = read_global(refs, core_ref)
        keys.append(k)
        values.append(v)
    return keys, values, core_ref


def slot_operands(near, parts, core):
    args, specs = [], []
    for k, v, row in near:
        rows = k.shape[0] if row == 0 else k.shape[0] // 2
        args += [k, v]
        specs += [column_block(rows, HD), column_block(rows, HD, row)]
    if parts:
        args += [core] + list(parts)
        specs += [SCALAR] + [column_block(x.shape[0], HD) for x in parts]
    slots = sum(k.shape[0] if row == 0 else k.shape[0] // 2 for k, _, row in near)
    return args, specs, slots + sum(x.shape[0] for x in parts) // 2


def prepare_kernel(keep_ref, k_ref, v_ref, out_ref):
    rows, width = k_ref.shape
    keep = jnp.broadcast_to(keep_ref[...].astype(F32), (HD, rows)).T
    for start in range(0, width, HD):
        here = slice(start, start + HD)
        k = jnp.where(keep == 1.0, k_ref[:, here].astype(F32), HIDDEN)
        out_ref[:rows, here] = k.astype(BF16)
    out_ref[rows:, :] = v_ref[...]


def prepare(keep_row, keys, values):
    rows, width = keys.shape
    return pl.pallas_call(
        prepare_kernel,
        grid=(1,),
        in_specs=[fixed_block(x.shape) for x in (keep_row, keys, values)],
        out_specs=WHOLE,
        out_shape=jax.ShapeDtypeStruct((2 * rows, width), BF16),
        compiler_params=params(),
        cost_estimate=cost(2**20, 4 * rows * width * 2),
        name="prepare_keys_values",
    )(off_chip(keep_row), off_chip(keys), off_chip(values))


def forward_kernel(near, parts, own, first, last, kept, resident, waits, *refs):
    refs = list(refs)
    take = refs.pop
    for _ in range(waits):
        take(0)
    q_ref = take(0)
    key_list, value_list, _ = read_slots(take, near, parts)
    keep_ref = take(0) if own else None
    if not first:
        sum_ref, peak_ref, total_ref = take(0), take(0), take(0)
    if last:
        cot_ref, gain_ref = take(0), take(0)
    p_refs = [take(0) for _ in kept]
    out_ref, peak_out, total_out = take(0), take(0), take(0)
    if last:
        rows_ref, square_acc, cross_acc = take(0), take(0), take(0)
        step = pl.program_id(0)

    rows = q_ref.shape[0]
    base = pl.multiple_of(pl.program_id(0) * (GROUP * rows), GROUP * rows)
    lanes = lane_of((rows, HD))
    unit = (lanes == 0).astype(BF16)
    wide_keys, wide_values = [], []
    for number, (k, v) in enumerate(zip(key_list, value_list)):
        if own and number == 0:
            extra = jnp.zeros_like(k)
        else:
            hidden = (lane_of(k.shape) == 0) & (k.astype(F32) > HIDDEN_ABOVE)
            extra = jnp.where(hidden, NEG_FILL, 0.0).astype(BF16)
        wide_keys.append(jnp.concatenate([k, extra], 1))
        wide_values.append(jnp.concatenate([v, jnp.ones_like(v)], 1))
    if own:
        square = (rows, rows)
        itself = lax.broadcasted_iota(jnp.int32, square, 0) == lane_of(square)
        visible = itself | (jnp.broadcast_to(keep_ref[...], square) == 1)

    def scores_of(head, number):
        q = jnp.concatenate([q_ref[:, head * HD : (head + 1) * HD], unit], 1)
        return dot_nt(q, wide_keys[number])

    def keep_exponentials(head, number, value):
        group = next(i for i, members in enumerate(kept) if number in members)
        start = sum(wide_keys[i].shape[0] for i in kept[group] if i < number)
        stop = start + wide_keys[number].shape[0]
        lower = base + head * rows if resident[group] else head * rows
        p_refs[group][pl.ds(lower, rows), start:stop] = value
        return dot_nn(value, wide_values[number])

    totals = jnp.ones((rows, HD), F32)
    order = [(head, number) for head in range(GROUP) for number in range(len(wide_keys))]
    ahead = scores_of(*order[0])
    mixed = None
    for place, (head, number) in enumerate(order):
        scores = ahead
        if place + 1 < len(order):
            ahead = scores_of(*order[place + 1])
        expo = jnp.exp2(scores * EXPONENT)
        if own and number == 0:
            expo = jnp.where(visible, expo, 0.0)
        part = keep_exponentials(head, number, expo.astype(BF16))
        mixed = part if number == 0 else mixed + part
        if number + 1 == len(wide_keys):
            here = slice(head * HD, (head + 1) * HD)
            value_sum, total = mixed[:, :HD], mixed[:, HD:]
            if not first:
                value_sum = value_sum + sum_ref[:, here]
                total = total + total_ref[:, head : head + 1]
            if last:
                total = 1.0 / total
                value_sum = value_sum * total
            out_ref[:, here] = value_sum
            totals = jnp.where(lanes == head, total, totals)
    total_out[...] = totals
    peak_out[...] = jnp.zeros((rows, HD), F32)
    if last:
        good = (totals >= 1.0 / TOTAL_MOST) & (totals <= 1.0 / TOTAL_LEAST)
    else:
        good = (totals >= TOTAL_LEAST) & (totals <= TOTAL_MOST)
    if not first:
        good = good & (peak_ref[...] == 0.0)
    in_range = jnp.min(jnp.where(good, 1.0, 0.0)) > 0.5

    @pl.when(jnp.logical_not(in_range))
    def _():
        peaks = jnp.zeros((rows, HD), F32)
        safe_totals = jnp.ones((rows, HD), F32)
        for head in range(GROUP):
            scores = [scores_of(head, number) for number in range(len(wide_keys))]
            if own:
                scores[0] = jnp.where(visible, scores[0], NEG_FILL)
            peak = functools.reduce(jnp.maximum, [jnp.max(s, -1, keepdims=True) for s in scores])
            if not first:
                before = peak_ref[:, head : head + 1]
                peak = jnp.maximum(peak, before)
            mix = None
            for number, s in enumerate(scores):
                e = jnp.exp2((s - peak) * EXPONENT).astype(BF16)
                part = keep_exponentials(head, number, e)
                mix = part if mix is None else mix + part
            here = slice(head * HD, (head + 1) * HD)
            value_sum, total = mix[:, :HD], mix[:, HD:]
            if not first:
                shrink = jnp.exp2((before - peak) * EXPONENT)
                value_sum = value_sum + sum_ref[:, here] * shrink
                total = total + total_ref[:, head : head + 1] * shrink
            if last:
                total = 1.0 / total
                value_sum = value_sum * total
            out_ref[:, here] = value_sum
            safe_totals = jnp.where(lanes == head, total, safe_totals)
            peaks = jnp.where(lanes == head, peak, peaks)
        peak_out[...] = peaks
        total_out[...] = safe_totals

    if last:

        @pl.when(step == 0)
        def _():
            square_acc[...] = jnp.zeros_like(square_acc)
            cross_acc[...] = jnp.zeros_like(cross_acc)

        squares, crosses = square_acc[...], cross_acc[...]
        for head in range(GROUP):
            here = slice(head * HD, (head + 1) * HD)
            attn = out_ref[:, here]
            upstream = cot_ref[:, here].astype(F32) * gain_ref[:, here].astype(F32)
            squares = squares + attn * attn
            crosses = crosses + upstream * attn
        square_acc[...] = squares
        cross_acc[...] = crosses

        @pl.when(step == pl.num_programs(0) - 1)
        def _():
            square_row = jnp.sum(square_acc[...].T, 0, keepdims=True)
            cross_row = jnp.sum(cross_acc[...].T, 0, keepdims=True)
            rows_ref[...] = jnp.concatenate([square_row, cross_row], 0)


def forward_phase(
    name, queries, near, parts=(), core=None, keep_row=None, before=None, norm=None, kept=None,
    resident=(False, False), after=(),
):
    rows, width = queries.shape
    steps = width // (GROUP * HD)
    wide = GROUP * HD
    args, specs, slots = slot_operands(near, parts, core)
    block_rows = [rows] * len(near) + ([slots - rows * len(near)] if parts else [])
    sizes = [slots] if kept is None else [sum(block_rows[i] for i in members) for members in kept]
    kept = [range(len(near) + 1)] if kept is None else kept
    args = list(after) + [queries] + args
    specs = [ANYWHERE] * len(after) + [column_block(rows, wide)] + specs
    if keep_row is not None:
        args.append(keep_row)
        specs.append(fixed_block(keep_row.shape))
    if before is not None:
        args += list(before)
        specs += [column_block(rows, wide), column_block(rows, HD), column_block(rows, HD)]
    if norm is not None:
        args += list(norm)
        specs += [column_block(rows, wide), column_block(1, wide)]
    place = jax.ShapeDtypeStruct if norm is None else pltpu.HBM
    out_shapes = [pltpu.HBM((steps * GROUP * rows, size), BF16) for size in sizes] + [
        place((rows, width), F32),
        jax.ShapeDtypeStruct((rows, steps * HD), F32),
        jax.ShapeDtypeStruct((rows, steps * HD), F32),
    ]
    out_specs = [
        WHOLE if stay else pl.BlockSpec((GROUP * rows, size), lambda a: (a, 0))
        for size, stay in zip(sizes, resident)
    ] + [
        column_block(rows, wide),
        column_block(rows, HD),
        column_block(rows, HD),
    ]
    scratch = []
    if norm is not None:
        out_shapes.append(jax.ShapeDtypeStruct((2, rows), F32))
        out_specs.append(fixed_block((2, rows)))
        scratch = [pltpu.VMEM((rows, HD), F32), pltpu.VMEM((rows, HD), F32)]
    elements = rows * slots * steps * GROUP
    return pl.pallas_call(
        functools.partial(
            forward_kernel, len(near), len(parts), keep_row is not None, before is None,
            norm is not None, kept, resident, len(after),
        ),
        grid=(steps,),
        in_specs=specs,
        out_specs=out_specs,
        out_shape=out_shapes,
        scratch_shapes=scratch,
        compiler_params=params(),
        cost_estimate=cost(8 * elements * HD, 2 * elements, elements),
        name=name,
    )(*args)


def backward_kernel(near, parts, own, later, last, features, added, resident, waits, *refs):
    refs = list(refs)
    take = refs.pop
    for _ in range(waits):
        take(0)
    first = later is not None
    q_ref, p_ref = take(0), take(0)
    key_list, value_list, core_ref = read_slots(take, near, parts)
    if first:
        peak_refs = [take(0) for _ in range(later + 1)]
        inverse_ref, norm_ref, other_ref, attn_ref, cot_ref, gain_ref = [take(0) for _ in range(6)]
    else:
        grad_ref, diag_ref, dq_ref = take(0), take(0), take(0)
    add_refs = [take(0) for _ in range(added)]
    outs = [take(0) for _ in range(near + parts)]
    dq_out = take(0)
    if first:
        normed_out = take(0)
        later_outs = [(take(0), take(0)) for _ in range(later)]
    ds_ref, q_stack, grad_stack = take(0), take(0), take(0)

    rows = q_ref.shape[0]
    base = 0
    if resident:
        base = pl.multiple_of(pl.program_id(0) * (GROUP * rows), GROUP * rows)
    lanes = lane_of((rows, HD))
    if first:
        inverse_total = inverse_ref[...]
        factors = [inverse_total] + [
            jnp.exp2((r[...] - peak_refs[0][...]) * EXPONENT) * inverse_total for r in peak_refs[1:]
        ]
        squares = norm_ref[0:1, :] + other_ref[0:1, :]
        crossed = norm_ref[1:2, :] + other_ref[1:2, :]
        inverse_row = lax.rsqrt(squares / features + NORM_EPS)
        coefficient_row = inverse_row * inverse_row * inverse_row * crossed / features
        inverse_wide = jnp.broadcast_to(inverse_row, (HD, rows)).T
        coefficient_wide = jnp.broadcast_to(coefficient_row, (HD, rows)).T
        diags = [jnp.zeros((rows, HD), F32)] * later

    gradients, diagonals = [], []
    for head in range(GROUP):
        here = slice(head * HD, (head + 1) * HD)
        stack = slice(head * rows, (head + 1) * rows)
        if first:
            attn = attn_ref[:, here]
            gain = gain_ref[:, here].astype(F32)
            normed_out[:, here] = (attn * inverse_wide * gain).astype(BF16)
            upstream = cot_ref[:, here].astype(F32) * gain
            grad = inverse_wide * upstream - attn * coefficient_wide
            diag = jnp.sum(grad * attn, -1, keepdims=True)
            factor = factors[0][:, head : head + 1]
            grad_bf = (grad * factor).astype(BF16)
            scaled_diag = diag * factor
            for number, (grad_out, _) in enumerate(later_outs):
                factor = factors[number + 1][:, head : head + 1]
                grad_out[:, here] = (grad * factor).astype(BF16)
                diags[number] = jnp.where(lanes == head, diag * factor, diags[number])
        else:
            grad_bf = grad_ref[:, here]
            scaled_diag = diag_ref[:, head : head + 1]
        grad_stack[stack, :] = grad_bf
        q_stack[stack, :] = q_ref[:, here]
        start = 0
        d_query = None
        for k, v in zip(key_list, value_list):
            columns = slice(start, start + k.shape[0])
            d_probs = dot_nt(grad_bf, v)
            d_scores = (p_ref[pl.ds(base + head * rows, rows), columns].astype(F32) * (d_probs - scaled_diag)).astype(BF16)
            ds_ref[stack, columns] = d_scores
            part = dot_nn(d_scores, k)
            d_query = part if d_query is None else d_query + part
            start += k.shape[0]
        if not first:
            d_query = d_query + dq_ref[:, here]
        if last:
            d_query = d_query * SCALING
        dq_out[:, here] = d_query.astype(dq_out.dtype)
    if first:
        for (_, diag_out), diag in zip(later_outs, diags):
            diag_out[...] = diag
    q_all, grad_all = q_stack[...], grad_stack[...]
    start = 0
    for number, k in enumerate(key_list):
        size = k.shape[0]
        columns = slice(start, start + size)
        start += size
        d_key = (dot_tn(q_all, ds_ref[:, columns]) * SCALING).T
        d_value = dot_tn(grad_all, p_ref[pl.ds(base, GROUP * rows), columns]).T
        if number < near:
            out = outs[number]
            if own and number == 0:
                for ref in add_refs:
                    d_key = d_key + ref[:size, :].astype(F32)
                    d_value = d_value + ref[size:, :].astype(F32)
            out[:size, :] = d_key.astype(out.dtype)
            out[size:, :] = d_value.astype(out.dtype)
        else:
            d_key, d_value = d_key.astype(BF16), d_value.astype(BF16)
            core_first = core_ref[0] == 0
            mine = jnp.where(core_first, d_key, d_value)
            other = jnp.where(core_first, d_value, d_key)
            begin = 0
            for part in range(parts // 2):
                mine_out, other_out = outs[near + part], outs[near + parts // 2 + part]
                length = mine_out.shape[0]
                mine_out[...] = mine[begin : begin + length]
                other_out[...] = other[begin : begin + length]
                begin += length


def backward_phase(
    name, queries, probs, near, parts=(), core=None, own=False, peaks=None, norm=None,
    grads=None, last=False, add=(), resident=False,
    after=(),
):
    rows, width = queries.shape
    steps = width // (GROUP * HD)
    wide = GROUP * HD
    slots = probs.shape[1]
    args, specs, _ = slot_operands(near, parts, core)
    args = list(after) + [queries, off_chip(probs)] + args
    specs = [ANYWHERE] * len(after) + [
        column_block(rows, wide),
        WHOLE if resident else pl.BlockSpec((GROUP * rows, slots), lambda a: (a, 0)),
    ] + specs
    out_shapes, out_specs = [], []
    for number, (k, _, row) in enumerate(near):
        size = k.shape[0] if row == 0 else k.shape[0] // 2
        kind = F32 if own and number == 0 else BF16
        out_shapes.append(jax.ShapeDtypeStruct((2 * size, k.shape[1]), kind))
        out_specs.append(column_block(2 * size, HD))
    for x in parts:
        out_shapes.append(jax.ShapeDtypeStruct(x.shape, BF16))
        out_specs.append(column_block(x.shape[0], HD))
    later = None
    if norm is not None:
        later = len(peaks) - 1
        inverse, sums, others, attn, cotangent, gain = norm
        args += list(peaks) + [inverse, sums, others, off_chip(attn), cotangent, gain]
        specs += [column_block(rows, HD)] * (len(peaks) + 1) + [
            fixed_block(sums.shape),
            fixed_block(others.shape),
            column_block(rows, wide),
            column_block(rows, wide),
            column_block(1, wide),
        ]
    else:
        args += list(grads)
        specs += [column_block(rows, wide), column_block(rows, HD), column_block(rows, wide)]
    args += list(add)
    specs += [column_block(x.shape[0], HD) for x in add]
    out_shapes.append(jax.ShapeDtypeStruct((rows, width), BF16 if last else F32))
    out_specs.append(column_block(rows, wide))
    if norm is not None:
        out_shapes.append(jax.ShapeDtypeStruct((rows, width), BF16))
        out_specs.append(column_block(rows, wide))
        for _ in range(later):
            out_shapes += [
                jax.ShapeDtypeStruct((rows, width), BF16),
                jax.ShapeDtypeStruct((rows, steps * HD), F32),
            ]
            out_specs += [column_block(rows, wide), column_block(rows, HD)]
    elements = rows * slots * steps * GROUP
    return pl.pallas_call(
        functools.partial(
            backward_kernel, len(near), len(parts), own, later, last, QH * HD, len(add), resident,
            len(after),
        ),
        grid=(steps,),
        in_specs=specs,
        out_specs=out_specs,
        out_shape=out_shapes,
        scratch_shapes=[
            pltpu.VMEM((GROUP * rows, slots), BF16),
            pltpu.VMEM((GROUP * rows, HD), BF16),
            pltpu.VMEM((GROUP * rows, HD), BF16),
        ],
        compiler_params=params(),
        cost_estimate=cost(12 * elements * HD, 2 * elements),
        name=name,
    )(*args)


def pick_kernel(core_ref, spots_ref, own_ref, partner_ref, *refs):
    out_refs = refs[2:]
    rows = own_ref.shape[0] // 2
    count = spots_ref.shape[1]
    first = core_ref[0] == 0
    row_ids = lax.broadcasted_iota(jnp.int32, (rows, count), 0)
    total = None
    for number, ref in enumerate((own_ref, partner_ref)):
        source = jnp.where(first, ref[:rows, :], ref[rows:, :])
        chosen = jnp.where(row_ids == spots_ref[number : number + 1, :], 1.0, 0.0).astype(BF16)
        part = dot_tn(chosen, source)
        total = part if total is None else total + part
    write_pieces(total, out_refs)


def write_pieces(total, out_refs):
    start = 0
    for ref in out_refs:
        ref[...] = total[start : start + ref.shape[0]].astype(ref.dtype)
        start += ref.shape[0]


def piece_shapes(count, rows, width):
    return [jax.ShapeDtypeStruct((rows // count, width), BF16)] * count


def pick(core, spots, own, partner, pieces):
    count, width = spots.shape[1], own.shape[1]
    return pl.pallas_call(
        pick_kernel,
        in_specs=[SCALAR] + [WHOLE] * 3 + [ANYWHERE],
        out_specs=[ANYWHERE] + [WHOLE] * pieces,
        out_shape=[jax.ShapeDtypeStruct(own.shape, own.dtype)] + piece_shapes(pieces, count, width),
        input_output_aliases={4: 0},
        compiler_params=params(),
        cost_estimate=cost(2 * count * width * own.shape[0], 3 * 2**20),
        name="pick_globals",
    )(core, spots, own, partner, own)


def combine_kernel(waits, blocks, *refs):
    blocks_in = refs[waits : waits + blocks]
    running = blocks_in[0][...].astype(F32)
    for ref in blocks_in[1:]:
        running = running + ref[...].astype(F32)
    write_pieces(running, refs[waits + blocks :])


def combine(blocks, pieces, after=()):
    rows, width = blocks[0].shape
    return pl.pallas_call(
        functools.partial(combine_kernel, len(after), len(blocks)),
        in_specs=[ANYWHERE] * len(after) + [WHOLE] * len(blocks),
        out_specs=[WHOLE] * pieces,
        out_shape=piece_shapes(pieces, rows, width),
        compiler_params=params(),
        cost_estimate=cost(2**20, len(blocks) * rows * width * 4),
        name="combine_globals",
    )(*after, *blocks)


def join_kernel(waits, blocks, *refs):
    out_ref = refs[-1]
    start = 0
    for ref in refs[waits : waits + blocks]:
        out_ref[start : start + ref.shape[0], :] = ref[...]
        start += ref.shape[0]


def join(blocks, after=()):
    rows = sum(x.shape[0] for x in blocks)
    width = blocks[0].shape[1]
    return pl.pallas_call(
        functools.partial(join_kernel, len(after), len(blocks)),
        in_specs=[ANYWHERE] * len(after) + [WHOLE] * len(blocks),
        out_specs=WHOLE,
        out_shape=jax.ShapeDtypeStruct((rows, width), BF16),
        compiler_params=params(),
        cost_estimate=cost(2**20, rows * width * 4),
        name="join_globals",
    )(*after, *blocks)


def settle_kernel(waits, *refs):
    own_ref, far_keys_ref, far_values_ref = refs[waits : waits + 3]
    refs = refs[waits + 3 : -3] + refs[-2:-1]
    rows = far_keys_ref.shape[0]
    for here, far_ref in ((slice(0, rows), far_keys_ref), (slice(rows, 2 * rows), far_values_ref)):
        running = own_ref[here, :] + far_ref[...].astype(F32)
        for ref in refs[:-1]:
            running = running + ref[here, :].astype(F32)
        refs[-1][here, :] = running


def settle(own, back, far_keys, far_values, through, after=()):
    return pl.pallas_call(
        functools.partial(settle_kernel, len(after)),
        in_specs=[ANYWHERE] * len(after) + [WHOLE] * (3 + len(back)) + [ANYWHERE],
        out_specs=[WHOLE, ANYWHERE],
        out_shape=[jax.ShapeDtypeStruct(x.shape, x.dtype) for x in (own, through)],
        input_output_aliases={len(after) + 3 + len(back): 1},
        compiler_params=params(),
        cost_estimate=cost(2**20, 4 * 2**20),
        name="settle_partner_grads",
    )(*after, own, far_keys, far_values, *back, through)


def finish_kernel(partners, parts, *refs):
    core_ref, spots_ref, own = refs[:3]
    back = refs[3 : 3 + partners]
    total = refs[3 + partners : 3 + partners + parts]
    outs = refs[3 + partners + parts :]
    rows = own.shape[0] // 2
    count = spots_ref.shape[1]
    row_ids = lax.broadcasted_iota(jnp.int32, (rows, count), 0)
    chosen = jnp.where(row_ids == spots_ref[0:1, :], 1.0, 0.0).astype(BF16)
    global_grads = read_global(total, core_ref)
    for kind in range(2):
        here = slice(kind * rows, (kind + 1) * rows)
        running = own[here, :]
        for ref in back:
            running = running + ref[here, :].astype(F32)
        running = running + dot_nn(chosen, global_grads[kind])
        outs[kind][...] = running.astype(BF16)


def finish(core, spots, own, back, total):
    args = [own] + list(back) + list(total)
    rows, width = own.shape
    return pl.pallas_call(
        functools.partial(finish_kernel, len(back), len(total)),
        in_specs=[SCALAR] + [WHOLE] * (len(args) + 1),
        out_specs=[WHOLE] * 2,
        out_shape=[jax.ShapeDtypeStruct((rows // 2, width), BF16)] * 2,
        compiler_params=params(),
        cost_estimate=cost(2**28, 4 * 2**20),
        name="finish_key_value_grads",
    )(core, spots, *args)


def levels_of(bit_count):
    bits = list(range(1, bit_count))
    levels = []
    while bits:
        levels.insert(0, bits[-2:])
        bits = bits[:-2]
    return levels


def masks_of(level):
    return [
        sum(1 << bit for place, bit in enumerate(level) if number >> place & 1)
        for number in range(1 << len(level))
    ]


def exchange(blocks, masks):
    return [blocks[0]] + [swap(x, "seq", mask) for x, mask in zip(blocks[1:], masks[1:])]


def spread(block, masks):
    return [block] + [swap(block, "seq", mask) for mask in masks[1:]]


def per_device(queries, keys, values, key_keep, global_positions, gain, cotangent):
    rows = queries.shape[0]
    bit_count = lax.axis_size("seq").bit_length() - 1
    place = lax.axis_index("seq")
    core = (place & 1).reshape(1)
    global_count = global_positions.shape[0]
    keep_row = key_keep.reshape(1, rows)
    gain_row = gain.reshape(1, -1)
    queries, cotangent = off_chip(queries), off_chip(cotangent)

    packed = prepare(keep_row, keys, values)
    near = [swap(packed, "seq", 1)]

    levels = [masks_of(level) for level in levels_of(bit_count)]
    order = [0]
    for masks in levels:
        order = [base ^ mask for base in order for mask in masks]
    pieces = len(order)
    chunk_ids = (place >> 1) ^ jnp.array([mask >> 1 for mask in order], jnp.int32)
    chunks = global_positions.reshape(pieces, global_count // pieces)
    match = chunk_ids[:, None] == jnp.arange(pieces, dtype=jnp.int32)[None, :]
    ordered = jnp.sum(jnp.where(match[:, :, None], chunks[None], 0), 1).reshape(global_count)
    spots = jnp.stack([ordered - place * rows, ordered - (place ^ 1) * rows])

    outer, inner = levels
    packed, *picked = pick(core, spots, packed, near[0], len(outer))
    moved = exchange(picked, outer)
    near += [swap(packed, "seq", 1 << bit) for bit in range(1, bit_count)]

    group_1 = [(off_chip(keys), off_chip(values), 0), (near[0], near[0], 1)]
    group_2 = [(x, x, 1) for x in near[1:-1]]
    group_3 = [(near[-1], near[-1], 1)]

    p_1, *state_1 = forward_phase("forward_own", queries, group_1, keep_row=keep_row, after=picked[-1:])
    summed = combine(moved, len(inner), after=state_1[2:])
    moved = exchange(summed, inner)
    p_2, *state_2 = forward_phase(
        "forward_partners", queries, group_2, before=state_1, after=summed[-1:]
    )
    (piece,) = combine(moved, 1, after=state_2[2:])
    half = join(spread(piece, inner))
    mine = spread(half, outer)
    global_parts = mine + [swap(part, "seq", 1) for part in mine]
    p_3, attn, peak_3, inverse, sums = forward_phase(
        "forward_globals", queries, group_3, global_parts, core, before=state_2,
        norm=(cotangent, gain_row),
    )
    head_bits = lax.axis_size("head").bit_length() - 1
    others = jnp.zeros_like(sums)
    for bit in range(head_bits):
        sums = sums + others if bit else sums
        others = swap(sums, "head", 1 << bit)

    count = len(global_parts)
    back_3, *rest = backward_phase(
        "backward_globals", queries, p_3, group_3, global_parts, core,
        peaks=[peak_3, state_2[1], state_1[1]], norm=(inverse, sums, others, attn, cotangent, gain_row),
    )
    global_grads, (d_query, normed, grad_2, diag_2, grad_1, diag_1) = rest[:count], rest[count:]
    kept, given = global_grads[: count // 2], global_grads[count // 2 :]
    reduced = [combine([a, swap(b, "seq", 1)], 1)[0] for a, b in zip(kept, given)]
    summed = combine(exchange(reduced, outer), len(inner))
    moved = exchange(summed, inner)
    far_mask = 1 << (bit_count - 1)
    far_keys = swap(back_3[:rows], "seq", far_mask)
    *back_2, d_query = backward_phase(
        "backward_partners", queries, p_2, group_2, grads=(grad_2, diag_2, d_query), after=summed[-1:]
    )
    (piece,) = combine(moved, 1, after=[d_query])
    moved = spread(piece, inner)
    half = join(moved)
    mine = spread(half, outer)
    far_values = swap(back_3[rows:], "seq", far_mask)
    own, back_first, d_query = backward_phase(
        "backward_own", queries, p_1, group_1, own=True, grads=(grad_1, diag_1, d_query), last=True,
        after=[half, far_keys],
    )
    back_2 = [swap(x, "seq", 2 << number) for number, x in enumerate(back_2)]
    own, back_first = settle(own, back_2, far_keys, far_values, back_first, after=mine[1:])
    total_parts = mine + [swap(part, "seq", 1) for part in mine]
    key_grad, value_grad = finish(core, spots, own, [swap(back_first, "seq", 1)], total_parts)
    return normed, d_query, key_grad, value_grad


def solution(mesh):
    placed = (
        P("seq", "head"),
        P("seq", "head"),
        P("seq", "head"),
        P("seq"),
        P(),
        P("head"),
        P("seq", "head"),
    )
    return jax.shard_map(
        per_device,
        mesh=mesh,
        in_specs=placed,
        out_specs=(P("seq", "head"), P("seq", "head"), P("seq", "head"), P("seq", "head")),
        check_vma=False,
    )
```

```python
import functools
import math

import jax
import jax.numpy as jnp
from jax import lax
from jax.experimental import pallas as pl
from jax.experimental.pallas import tpu as pltpu
from jax.sharding import PartitionSpec as P

QH = 64
KVH = 8
HD = 128
GROUP = QH // KVH

NEG_FILL = -1e30
NORM_EPS = 1e-06
HIDDEN = 256.0
HIDDEN_ABOVE = 100.0
SCALING = HD ** (-0.5)
EXPONENT = SCALING * math.log2(math.e)
VMEM_BYTES = 28 * 2**20
FAR_STAYS = False
GLOBALS_STAY = False
AHEAD = 2
TOTAL_LEAST = 2.0**-80
TOTAL_MOST = 2.0**100

F32 = jnp.float32
BF16 = jnp.bfloat16


def dot_nt(left, right):
    return lax.dot_general(left, right, (((1,), (1,)), ((), ())), preferred_element_type=F32)


def dot_nn(left, right):
    return lax.dot_general(left, right, (((1,), (0,)), ((), ())), preferred_element_type=F32)


def dot_tn(left, right):
    return lax.dot_general(left, right, (((0,), (0,)), ((), ())), preferred_element_type=F32)


def swap(block, axis, mask):
    count = lax.axis_size(axis)
    return lax.ppermute(block, axis, [(i, i ^ mask) for i in range(count)])


def off_chip(block):
    return pltpu.with_memory_space_constraint(block, pltpu.HBM)


def params():
    return pltpu.CompilerParams(vmem_limit_bytes=VMEM_BYTES)


def cost(flops, moved, expos=0):
    return pl.CostEstimate(flops=int(flops), bytes_accessed=int(moved), transcendentals=int(expos))


def lane_of(shape):
    return lax.broadcasted_iota(jnp.int32, shape, 1)


def column_block(rows, width, row=0):
    return pl.BlockSpec((rows, width), lambda a: (row, a))


def fixed_block(shape):
    return pl.BlockSpec(shape, lambda a: (0,) * len(shape))


SCALAR = pl.BlockSpec(memory_space=pltpu.SMEM)
WHOLE = pl.BlockSpec(memory_space=pltpu.VMEM)
ANYWHERE = pl.BlockSpec(memory_space=pl.ANY)


def read_global(refs, core_ref):
    count = len(refs) // 2
    mine = jnp.concatenate([r[...] for r in refs[:count]], 0)
    other = jnp.concatenate([r[...] for r in refs[count:]], 0)
    first = core_ref[0] == 0
    return jnp.where(first, mine, other), jnp.where(first, other, mine)


def read_slots(take, near, parts):
    keys, values = [], []
    for _ in range(near):
        keys.append(take(0)[...])
        values.append(take(0)[...])
    core_ref = None
    if parts:
        core_ref = take(0)
        refs = [take(0) for _ in range(parts)]
        k, v = read_global(refs, core_ref)
        keys.append(k)
        values.append(v)
    return keys, values, core_ref


def slot_operands(near, parts, core):
    args, specs = [], []
    for k, v, row in near:
        rows = k.shape[0] if row == 0 else k.shape[0] // 2
        args += [k, v]
        specs += [column_block(rows, HD), column_block(rows, HD, row)]
    if parts:
        args += [core] + list(parts)
        specs += [SCALAR] + [column_block(x.shape[0], HD) for x in parts]
    slots = sum(k.shape[0] if row == 0 else k.shape[0] // 2 for k, _, row in near)
    return args, specs, slots + sum(x.shape[0] for x in parts) // 2


def prepare_kernel(keep_ref, k_ref, v_ref, out_ref):
    rows, width = k_ref.shape
    keep = jnp.broadcast_to(keep_ref[...].astype(F32), (HD, rows)).T
    for start in range(0, width, HD):
        here = slice(start, start + HD)
        k = jnp.where(keep == 1.0, k_ref[:, here].astype(F32), HIDDEN)
        out_ref[:rows, here] = k.astype(BF16)
    out_ref[rows:, :] = v_ref[...]


def prepare(keep_row, keys, values):
    rows, width = keys.shape
    return pl.pallas_call(
        prepare_kernel,
        grid=(1,),
        in_specs=[fixed_block(x.shape) for x in (keep_row, keys, values)],
        out_specs=WHOLE,
        out_shape=jax.ShapeDtypeStruct((2 * rows, width), BF16),
        compiler_params=params(),
        cost_estimate=cost(2**20, 4 * rows * width * 2),
        name="prepare_keys_values",
    )(keep_row, off_chip(keys), off_chip(values))


def forward_kernel(near, parts, own, first, last, kept, resident, waits, *refs):
    refs = list(refs)
    take = refs.pop
    for _ in range(waits):
        take(0)
    q_ref = take(0)
    key_list, value_list, _ = read_slots(take, near, parts)
    keep_ref = take(0) if own else None
    if not first:
        sum_ref, peak_ref, total_ref = take(0), take(0), take(0)
    if last:
        cot_ref, gain_ref = take(0), take(0)
    p_refs = [take(0) for _ in kept]
    out_ref, peak_out, total_out = take(0), take(0), take(0)
    if last:
        rows_ref, square_acc, cross_acc = take(0), take(0), take(0)
        step = pl.program_id(0)

    rows = q_ref.shape[0]
    base = pl.multiple_of(pl.program_id(0) * (GROUP * rows), GROUP * rows)
    lanes = lane_of((rows, HD))
    unit = (lanes == 0).astype(BF16)
    wide_keys, wide_values = [], []
    for number, (k, v) in enumerate(zip(key_list, value_list)):
        if own and number == 0:
            extra = jnp.zeros_like(k)
        else:
            hidden = (lane_of(k.shape) == 0) & (k.astype(F32) > HIDDEN_ABOVE)
            extra = jnp.where(hidden, NEG_FILL, 0.0).astype(BF16)
        wide_keys.append(jnp.concatenate([k, extra], 1))
        wide_values.append(jnp.concatenate([v, jnp.ones_like(v)], 1))
    if own:
        square = (rows, rows)
        itself = lax.broadcasted_iota(jnp.int32, square, 0) == lane_of(square)
        visible = itself | (jnp.broadcast_to(keep_ref[...], square) == 1)

    def scores_of(head, number):
        q = jnp.concatenate([q_ref[:, head * HD : (head + 1) * HD], unit], 1)
        return dot_nt(q, wide_keys[number])

    def keep_exponentials(head, number, value):
        group = next(i for i, members in enumerate(kept) if number in members)
        start = sum(wide_keys[i].shape[0] for i in kept[group] if i < number)
        stop = start + wide_keys[number].shape[0]
        lower = base + head * rows if resident[group] else head * rows
        p_refs[group][pl.ds(lower, rows), start:stop] = value
        return dot_nn(value, wide_values[number])

    totals = jnp.ones((rows, HD), F32)
    order = [(head, number) for head in range(GROUP) for number in range(len(wide_keys))]
    ahead = [scores_of(*step) for step in order[:AHEAD]]
    mixed = None
    for place, (head, number) in enumerate(order):
        scores = ahead.pop(0)
        if place + AHEAD < len(order):
            ahead.append(scores_of(*order[place + AHEAD]))
        expo = jnp.exp2(scores * EXPONENT)
        if own and number == 0:
            expo = jnp.where(visible, expo, 0.0)
        part = keep_exponentials(head, number, expo.astype(BF16))
        mixed = part if number == 0 else mixed + part
        if number + 1 == len(wide_keys):
            here = slice(head * HD, (head + 1) * HD)
            value_sum, total = mixed[:, :HD], mixed[:, HD:]
            if not first:
                value_sum = value_sum + sum_ref[:, here]
                total = total + total_ref[:, head : head + 1]
            if last:
                total = 1.0 / total
                value_sum = value_sum * total
            out_ref[:, here] = value_sum
            totals = jnp.where(lanes == head, total, totals)
    total_out[...] = totals
    peak_out[...] = jnp.zeros((rows, HD), F32)
    if last:
        good = (totals >= 1.0 / TOTAL_MOST) & (totals <= 1.0 / TOTAL_LEAST)
    else:
        good = (totals >= TOTAL_LEAST) & (totals <= TOTAL_MOST)
    if not first:
        good = good & (peak_ref[...] == 0.0)
    in_range = jnp.min(jnp.where(good, 1.0, 0.0)) > 0.5

    @pl.when(jnp.logical_not(in_range))
    def _():
        peaks = jnp.zeros((rows, HD), F32)
        safe_totals = jnp.ones((rows, HD), F32)
        for head in range(GROUP):
            scores = [scores_of(head, number) for number in range(len(wide_keys))]
            if own:
                scores[0] = jnp.where(visible, scores[0], NEG_FILL)
            peak = functools.reduce(jnp.maximum, [jnp.max(s, -1, keepdims=True) for s in scores])
            if not first:
                before = peak_ref[:, head : head + 1]
                peak = jnp.maximum(peak, before)
            mix = None
            for number, s in enumerate(scores):
                e = jnp.exp2((s - peak) * EXPONENT).astype(BF16)
                part = keep_exponentials(head, number, e)
                mix = part if mix is None else mix + part
            here = slice(head * HD, (head + 1) * HD)
            value_sum, total = mix[:, :HD], mix[:, HD:]
            if not first:
                shrink = jnp.exp2((before - peak) * EXPONENT)
                value_sum = value_sum + sum_ref[:, here] * shrink
                total = total + total_ref[:, head : head + 1] * shrink
            if last:
                total = 1.0 / total
                value_sum = value_sum * total
            out_ref[:, here] = value_sum
            safe_totals = jnp.where(lanes == head, total, safe_totals)
            peaks = jnp.where(lanes == head, peak, peaks)
        peak_out[...] = peaks
        total_out[...] = safe_totals

    if last:

        @pl.when(step == 0)
        def _():
            square_acc[...] = jnp.zeros_like(square_acc)
            cross_acc[...] = jnp.zeros_like(cross_acc)

        squares, crosses = square_acc[...], cross_acc[...]
        for head in range(GROUP):
            here = slice(head * HD, (head + 1) * HD)
            attn = out_ref[:, here]
            upstream = cot_ref[:, here].astype(F32) * gain_ref[:, here].astype(F32)
            squares = squares + attn * attn
            crosses = crosses + upstream * attn
        square_acc[...] = squares
        cross_acc[...] = crosses

        @pl.when(step == pl.num_programs(0) - 1)
        def _():
            square_row = jnp.sum(square_acc[...].T, 0, keepdims=True)
            cross_row = jnp.sum(cross_acc[...].T, 0, keepdims=True)
            rows_ref[...] = jnp.concatenate([square_row, cross_row], 0)


def forward_phase(
    name, queries, near, parts=(), core=None, keep_row=None, before=None, norm=None, kept=None,
    resident=(False, False), after=(),
):
    rows, width = queries.shape
    steps = width // (GROUP * HD)
    wide = GROUP * HD
    args, specs, slots = slot_operands(near, parts, core)
    block_rows = [rows] * len(near) + ([slots - rows * len(near)] if parts else [])
    sizes = [slots] if kept is None else [sum(block_rows[i] for i in members) for members in kept]
    kept = [range(len(near) + 1)] if kept is None else kept
    args = list(after) + [queries] + args
    specs = [ANYWHERE] * len(after) + [column_block(rows, wide)] + specs
    if keep_row is not None:
        args.append(keep_row)
        specs.append(fixed_block(keep_row.shape))
    if before is not None:
        args += list(before)
        specs += [column_block(rows, wide), column_block(rows, HD), column_block(rows, HD)]
    if norm is not None:
        args += list(norm)
        specs += [column_block(rows, wide), column_block(1, wide)]
    place = jax.ShapeDtypeStruct if norm is None else pltpu.HBM
    out_shapes = [pltpu.HBM((steps * GROUP * rows, size), BF16) for size in sizes] + [
        place((rows, width), F32),
        jax.ShapeDtypeStruct((rows, steps * HD), F32),
        jax.ShapeDtypeStruct((rows, steps * HD), F32),
    ]
    out_specs = [
        WHOLE if stay else pl.BlockSpec((GROUP * rows, size), lambda a: (a, 0))
        for size, stay in zip(sizes, resident)
    ] + [
        column_block(rows, wide),
        column_block(rows, HD),
        column_block(rows, HD),
    ]
    scratch = []
    if norm is not None:
        out_shapes.append(jax.ShapeDtypeStruct((2, rows), F32))
        out_specs.append(fixed_block((2, rows)))
        scratch = [pltpu.VMEM((rows, HD), F32), pltpu.VMEM((rows, HD), F32)]
    elements = rows * slots * steps * GROUP
    return pl.pallas_call(
        functools.partial(
            forward_kernel, len(near), len(parts), keep_row is not None, before is None,
            norm is not None, kept, resident, len(after),
        ),
        grid=(steps,),
        in_specs=specs,
        out_specs=out_specs,
        out_shape=out_shapes,
        scratch_shapes=scratch,
        compiler_params=params(),
        cost_estimate=cost(8 * elements * HD, 2 * elements, elements),
        name=name,
    )(*args)


def backward_kernel(near, parts, own, later, last, features, added, resident, waits, *refs):
    refs = list(refs)
    take = refs.pop
    for _ in range(waits):
        take(0)
    first = later is not None
    q_ref, p_ref = take(0), take(0)
    key_list, value_list, core_ref = read_slots(take, near, parts)
    if first:
        peak_refs = [take(0) for _ in range(later + 1)]
        inverse_ref, norm_ref, other_ref, attn_ref, cot_ref, gain_ref = [take(0) for _ in range(6)]
    else:
        grad_ref, diag_ref, dq_ref = take(0), take(0), take(0)
    add_refs = [take(0) for _ in range(added)]
    outs = [take(0) for _ in range(near + parts)]
    dq_out = take(0)
    if first:
        normed_out = take(0)
        later_outs = [(take(0), take(0)) for _ in range(later)]
    ds_ref, q_stack, grad_stack = take(0), take(0), take(0)

    rows = q_ref.shape[0]
    base = 0
    if resident:
        base = pl.multiple_of(pl.program_id(0) * (GROUP * rows), GROUP * rows)
    lanes = lane_of((rows, HD))
    if first:
        inverse_total = inverse_ref[...]
        factors = [inverse_total] + [
            jnp.exp2((r[...] - peak_refs[0][...]) * EXPONENT) * inverse_total for r in peak_refs[1:]
        ]
        squares = norm_ref[0:1, :] + other_ref[0:1, :]
        crossed = norm_ref[1:2, :] + other_ref[1:2, :]
        inverse_row = lax.rsqrt(squares / features + NORM_EPS)
        coefficient_row = inverse_row * inverse_row * inverse_row * crossed / features
        inverse_wide = jnp.broadcast_to(inverse_row, (HD, rows)).T
        coefficient_wide = jnp.broadcast_to(coefficient_row, (HD, rows)).T
        diags = [jnp.zeros((rows, HD), F32)] * later

    gradients, diagonals = [], []

    def read_head(head):
        here = slice(head * HD, (head + 1) * HD)
        stack = slice(head * rows, (head + 1) * rows)
        if first:
            attn = attn_ref[:, here]
            gain = gain_ref[:, here].astype(F32)
            normed_out[:, here] = (attn * inverse_wide * gain).astype(BF16)
            upstream = cot_ref[:, here].astype(F32) * gain
            grad = inverse_wide * upstream - attn * coefficient_wide
            diag = jnp.sum(grad * attn, -1, keepdims=True)
            factor = factors[0][:, head : head + 1]
            grad_bf = (grad * factor).astype(BF16)
            scaled_diag = diag * factor
            for number, (grad_out, _) in enumerate(later_outs):
                factor = factors[number + 1][:, head : head + 1]
                grad_out[:, here] = (grad * factor).astype(BF16)
                diags[number] = jnp.where(lanes == head, diag * factor, diags[number])
        else:
            grad_bf = grad_ref[:, here]
            scaled_diag = diag_ref[:, head : head + 1]
        grad_stack[stack, :] = grad_bf
        q_stack[stack, :] = q_ref[:, here]
        gradients.append(grad_bf)
        diagonals.append(scaled_diag)

    def d_probs_of(head, number):
        if first:
            return dot_nt(gradients[head], value_list[number])
        return dot_nt(grad_stack[head * rows : (head + 1) * rows, :], value_list[number])

    order = [(head, number) for head in range(GROUP) for number in range(len(key_list))]
    if not first:
        for head in range(GROUP):
            read_head(head)
        ahead = [d_probs_of(*step) for step in order[:AHEAD]]
    d_query = None
    for place, (head, number) in enumerate(order):
        if first:
            if number == 0:
                read_head(head)
            d_probs = d_probs_of(head, number)
        else:
            d_probs = ahead.pop(0)
            if place + AHEAD < len(order):
                ahead.append(d_probs_of(*order[place + AHEAD]))
        here = slice(head * HD, (head + 1) * HD)
        stack = slice(head * rows, (head + 1) * rows)
        k = key_list[number]
        start = sum(x.shape[0] for x in key_list[:number])
        columns = slice(start, start + k.shape[0])
        exponentials = p_ref[pl.ds(base + head * rows, rows), columns].astype(F32)
        d_scores = (exponentials * (d_probs - diagonals[head])).astype(BF16)
        ds_ref[stack, columns] = d_scores
        part = dot_nn(d_scores, k)
        d_query = part if number == 0 else d_query + part
        if number + 1 == len(key_list):
            if not first:
                d_query = d_query + dq_ref[:, here]
            if last:
                d_query = d_query * SCALING
            dq_out[:, here] = d_query.astype(dq_out.dtype)
    if first:
        for (_, diag_out), diag in zip(later_outs, diags):
            diag_out[...] = diag
    q_all, grad_all = q_stack[...], grad_stack[...]
    start = 0
    for number, k in enumerate(key_list):
        size = k.shape[0]
        columns = slice(start, start + size)
        start += size
        d_key = (dot_tn(q_all, ds_ref[:, columns]) * SCALING).T
        d_value = dot_tn(grad_all, p_ref[pl.ds(base, GROUP * rows), columns]).T
        if number < near:
            out = outs[number]
            if own and number == 0:
                for ref in add_refs:
                    d_key = d_key + ref[:size, :].astype(F32)
                    d_value = d_value + ref[size:, :].astype(F32)
            out[:size, :] = d_key.astype(out.dtype)
            out[size:, :] = d_value.astype(out.dtype)
        else:
            d_key, d_value = d_key.astype(BF16), d_value.astype(BF16)
            core_first = core_ref[0] == 0
            mine = jnp.where(core_first, d_key, d_value)
            other = jnp.where(core_first, d_value, d_key)
            begin = 0
            for part in range(parts // 2):
                mine_out, other_out = outs[near + part], outs[near + parts // 2 + part]
                length = mine_out.shape[0]
                mine_out[...] = mine[begin : begin + length]
                other_out[...] = other[begin : begin + length]
                begin += length


def backward_phase(
    name, queries, probs, near, parts=(), core=None, own=False, peaks=None, norm=None,
    grads=None, last=False, add=(), resident=False,
    after=(),
):
    rows, width = queries.shape
    steps = width // (GROUP * HD)
    wide = GROUP * HD
    slots = probs.shape[1]
    args, specs, _ = slot_operands(near, parts, core)
    args = list(after) + [queries, off_chip(probs)] + args
    specs = [ANYWHERE] * len(after) + [
        column_block(rows, wide),
        WHOLE if resident else pl.BlockSpec((GROUP * rows, slots), lambda a: (a, 0)),
    ] + specs
    out_shapes, out_specs = [], []
    for number, (k, _, row) in enumerate(near):
        size = k.shape[0] if row == 0 else k.shape[0] // 2
        kind = F32 if own and number == 0 else BF16
        out_shapes.append(jax.ShapeDtypeStruct((2 * size, k.shape[1]), kind))
        out_specs.append(column_block(2 * size, HD))
    for x in parts:
        out_shapes.append(jax.ShapeDtypeStruct(x.shape, BF16))
        out_specs.append(column_block(x.shape[0], HD))
    later = None
    if norm is not None:
        later = len(peaks) - 1
        inverse, sums, others, attn, cotangent, gain = norm
        args += list(peaks) + [inverse, sums, others, off_chip(attn), cotangent, gain]
        specs += [column_block(rows, HD)] * (len(peaks) + 1) + [
            fixed_block(sums.shape),
            fixed_block(others.shape),
            column_block(rows, wide),
            column_block(rows, wide),
            column_block(1, wide),
        ]
    else:
        args += list(grads)
        specs += [column_block(rows, wide), column_block(rows, HD), column_block(rows, wide)]
    args += list(add)
    specs += [column_block(x.shape[0], HD) for x in add]
    out_shapes.append(jax.ShapeDtypeStruct((rows, width), BF16 if last else F32))
    out_specs.append(column_block(rows, wide))
    if norm is not None:
        out_shapes.append(jax.ShapeDtypeStruct((rows, width), BF16))
        out_specs.append(column_block(rows, wide))
        for _ in range(later):
            out_shapes += [
                jax.ShapeDtypeStruct((rows, width), BF16),
                jax.ShapeDtypeStruct((rows, steps * HD), F32),
            ]
            out_specs += [column_block(rows, wide), column_block(rows, HD)]
    elements = rows * slots * steps * GROUP
    return pl.pallas_call(
        functools.partial(
            backward_kernel, len(near), len(parts), own, later, last, QH * HD, len(add), resident,
            len(after),
        ),
        grid=(steps,),
        in_specs=specs,
        out_specs=out_specs,
        out_shape=out_shapes,
        scratch_shapes=[
            pltpu.VMEM((GROUP * rows, slots), BF16),
            pltpu.VMEM((GROUP * rows, HD), BF16),
            pltpu.VMEM((GROUP * rows, HD), BF16),
        ],
        compiler_params=params(),
        cost_estimate=cost(12 * elements * HD, 2 * elements),
        name=name,
    )(*args)


def pick_kernel(core_ref, spots_ref, own_ref, partner_ref, *refs):
    out_refs = refs[2:]
    rows = own_ref.shape[0] // 2
    count = spots_ref.shape[1]
    first = core_ref[0] == 0
    row_ids = lax.broadcasted_iota(jnp.int32, (rows, count), 0)
    total = None
    for number, ref in enumerate((own_ref, partner_ref)):
        source = jnp.where(first, ref[:rows, :], ref[rows:, :])
        chosen = jnp.where(row_ids == spots_ref[number : number + 1, :], 1.0, 0.0).astype(BF16)
        part = dot_tn(chosen, source)
        total = part if total is None else total + part
    write_pieces(total, out_refs)


def write_pieces(total, out_refs):
    start = 0
    for ref in out_refs:
        ref[...] = total[start : start + ref.shape[0]].astype(ref.dtype)
        start += ref.shape[0]


def piece_shapes(count, rows, width):
    return [jax.ShapeDtypeStruct((rows // count, width), BF16)] * count


def pick(core, spots, own, partner, pieces):
    count, width = spots.shape[1], own.shape[1]
    return pl.pallas_call(
        pick_kernel,
        in_specs=[SCALAR] + [WHOLE] * 3 + [ANYWHERE],
        out_specs=[ANYWHERE] + [WHOLE] * pieces,
        out_shape=[jax.ShapeDtypeStruct(own.shape, own.dtype)] + piece_shapes(pieces, count, width),
        input_output_aliases={4: 0},
        compiler_params=params(),
        cost_estimate=cost(2 * count * width * own.shape[0], 3 * 2**20),
        name="pick_globals",
    )(core, spots, own, partner, own)


def combine_kernel(waits, blocks, *refs):
    blocks_in = refs[waits : waits + blocks]
    running = blocks_in[0][...].astype(F32)
    for ref in blocks_in[1:]:
        running = running + ref[...].astype(F32)
    write_pieces(running, refs[waits + blocks :])


def combine(blocks, pieces, after=()):
    rows, width = blocks[0].shape
    return pl.pallas_call(
        functools.partial(combine_kernel, len(after), len(blocks)),
        in_specs=[ANYWHERE] * len(after) + [WHOLE] * len(blocks),
        out_specs=[WHOLE] * pieces,
        out_shape=piece_shapes(pieces, rows, width),
        compiler_params=params(),
        cost_estimate=cost(2**20, len(blocks) * rows * width * 4),
        name="combine_globals",
    )(*after, *blocks)


def join_kernel(waits, blocks, *refs):
    out_ref = refs[-1]
    start = 0
    for ref in refs[waits : waits + blocks]:
        out_ref[start : start + ref.shape[0], :] = ref[...]
        start += ref.shape[0]


def join(blocks, after=()):
    rows = sum(x.shape[0] for x in blocks)
    width = blocks[0].shape[1]
    return pl.pallas_call(
        functools.partial(join_kernel, len(after), len(blocks)),
        in_specs=[ANYWHERE] * len(after) + [WHOLE] * len(blocks),
        out_specs=WHOLE,
        out_shape=jax.ShapeDtypeStruct((rows, width), BF16),
        compiler_params=params(),
        cost_estimate=cost(2**20, rows * width * 4),
        name="join_globals",
    )(*after, *blocks)


def settle_kernel(waits, *refs):
    own_ref, far_keys_ref, far_values_ref = refs[waits : waits + 3]
    refs = refs[waits + 3 : -3] + refs[-2:-1]
    rows = far_keys_ref.shape[0]
    for here, far_ref in ((slice(0, rows), far_keys_ref), (slice(rows, 2 * rows), far_values_ref)):
        running = own_ref[here, :] + far_ref[...].astype(F32)
        for ref in refs[:-1]:
            running = running + ref[here, :].astype(F32)
        refs[-1][here, :] = running


def settle(own, back, far_keys, far_values, through, after=()):
    return pl.pallas_call(
        functools.partial(settle_kernel, len(after)),
        in_specs=[ANYWHERE] * len(after) + [WHOLE] * (3 + len(back)) + [ANYWHERE],
        out_specs=[WHOLE, ANYWHERE],
        out_shape=[jax.ShapeDtypeStruct(x.shape, x.dtype) for x in (own, through)],
        input_output_aliases={len(after) + 3 + len(back): 1},
        compiler_params=params(),
        cost_estimate=cost(2**20, 4 * 2**20),
        name="settle_partner_grads",
    )(*after, own, far_keys, far_values, *back, through)


def finish_kernel(partners, parts, *refs):
    core_ref, spots_ref, own = refs[:3]
    back = refs[3 : 3 + partners]
    total = refs[3 + partners : 3 + partners + parts]
    outs = refs[3 + partners + parts :]
    rows = own.shape[0] // 2
    count = spots_ref.shape[1]
    row_ids = lax.broadcasted_iota(jnp.int32, (rows, count), 0)
    chosen = jnp.where(row_ids == spots_ref[0:1, :], 1.0, 0.0).astype(BF16)
    global_grads = read_global(total, core_ref)
    for kind in range(2):
        here = slice(kind * rows, (kind + 1) * rows)
        running = own[here, :]
        for ref in back:
            running = running + ref[here, :].astype(F32)
        running = running + dot_nn(chosen, global_grads[kind])
        outs[kind][...] = running.astype(BF16)


def finish(core, spots, own, back, total):
    args = [own] + list(back) + list(total)
    rows, width = own.shape
    return pl.pallas_call(
        functools.partial(finish_kernel, len(back), len(total)),
        in_specs=[SCALAR] + [WHOLE] * (len(args) + 1),
        out_specs=[WHOLE] * 2,
        out_shape=[jax.ShapeDtypeStruct((rows // 2, width), BF16)] * 2,
        compiler_params=params(),
        cost_estimate=cost(2**28, 4 * 2**20),
        name="finish_key_value_grads",
    )(core, spots, *args)


def levels_of(bit_count):
    bits = list(range(1, bit_count))
    levels = []
    while bits:
        levels.insert(0, bits[-2:])
        bits = bits[:-2]
    return levels


def masks_of(level):
    return [
        sum(1 << bit for place, bit in enumerate(level) if number >> place & 1)
        for number in range(1 << len(level))
    ]


def exchange(blocks, masks):
    return [blocks[0]] + [swap(x, "seq", mask) for x, mask in zip(blocks[1:], masks[1:])]


def spread(block, masks):
    return [block] + [swap(block, "seq", mask) for mask in masks[1:]]


def per_device(queries, keys, values, key_keep, global_positions, gain, cotangent):
    rows = queries.shape[0]
    bit_count = lax.axis_size("seq").bit_length() - 1
    place = lax.axis_index("seq")
    core = (place & 1).reshape(1)
    global_count = global_positions.shape[0]
    keep_row = off_chip(key_keep.reshape(1, rows))
    gain_row = gain.reshape(1, -1)
    queries, cotangent = off_chip(queries), off_chip(cotangent)

    packed = prepare(keep_row, keys, values)
    near = [swap(packed, "seq", 1)]

    levels = [masks_of(level) for level in levels_of(bit_count)]
    order = [0]
    for masks in levels:
        order = [base ^ mask for base in order for mask in masks]
    pieces = len(order)
    chunk_ids = (place >> 1) ^ jnp.array([mask >> 1 for mask in order], jnp.int32)
    chunks = global_positions.reshape(pieces, global_count // pieces)
    match = chunk_ids[:, None] == jnp.arange(pieces, dtype=jnp.int32)[None, :]
    ordered = jnp.sum(jnp.where(match[:, :, None], chunks[None], 0), 1).reshape(global_count)
    spots = jnp.stack([ordered - place * rows, ordered - (place ^ 1) * rows])

    outer, inner = levels
    packed, *picked = pick(core, spots, packed, near[0], len(outer))
    moved = exchange(picked, outer)
    near += [swap(packed, "seq", 1 << bit) for bit in range(1, bit_count)]

    group_1 = [(off_chip(keys), off_chip(values), 0), (near[0], near[0], 1)]
    group_2 = [(x, x, 1) for x in near[1:-1]]
    group_3 = [(near[-1], near[-1], 1)]

    p_1, *state_1 = forward_phase("forward_own", queries, group_1, keep_row=keep_row, after=picked[-1:])
    summed = combine(moved, len(inner), after=state_1[2:])
    moved = exchange(summed, inner)
    p_2, *state_2 = forward_phase(
        "forward_partners", queries, group_2, before=state_1, after=summed[-1:]
    )
    (piece,) = combine(moved, 1, after=state_2[2:])
    half = join(spread(piece, inner))
    mine = spread(half, outer)
    global_parts = mine + [swap(part, "seq", 1) for part in mine]
    p_3, attn, peak_3, inverse, sums = forward_phase(
        "forward_globals", queries, group_3, global_parts, core, before=state_2,
        norm=(cotangent, gain_row),
    )
    head_bits = lax.axis_size("head").bit_length() - 1
    others = jnp.zeros_like(sums)
    for bit in range(head_bits):
        sums = sums + others if bit else sums
        others = swap(sums, "head", 1 << bit)

    count = len(global_parts)
    back_3, *rest = backward_phase(
        "backward_globals", queries, p_3, group_3, global_parts, core,
        peaks=[peak_3, state_2[1], state_1[1]], norm=(inverse, sums, others, attn, cotangent, gain_row),
    )
    global_grads, (d_query, normed, grad_2, diag_2, grad_1, diag_1) = rest[:count], rest[count:]
    kept, given = global_grads[: count // 2], global_grads[count // 2 :]
    reduced = [combine([a, swap(b, "seq", 1)], 1)[0] for a, b in zip(kept, given)]
    summed = combine(exchange(reduced, outer), len(inner))
    moved = exchange(summed, inner)
    far_mask = 1 << (bit_count - 1)
    far_keys = swap(back_3[:rows], "seq", far_mask)
    *back_2, d_query = backward_phase(
        "backward_partners", queries, p_2, group_2, grads=(grad_2, diag_2, d_query), after=summed[-1:]
    )
    (piece,) = combine(moved, 1, after=[d_query])
    moved = spread(piece, inner)
    half = join(moved)
    mine = spread(half, outer)
    far_values = swap(back_3[rows:], "seq", far_mask)
    own, back_first, d_query = backward_phase(
        "backward_own", queries, p_1, group_1, own=True, grads=(grad_1, diag_1, d_query), last=True,
        after=[half, far_keys],
    )
    back_2 = [swap(x, "seq", 2 << number) for number, x in enumerate(back_2)]
    own, back_first = settle(own, back_2, far_keys, far_values, back_first, after=mine[1:])
    total_parts = mine + [swap(part, "seq", 1) for part in mine]
    key_grad, value_grad = finish(core, spots, own, [swap(back_first, "seq", 1)], total_parts)
    return normed, d_query, key_grad, value_grad


def solution(mesh):
    placed = (
        P("seq", "head"),
        P("seq", "head"),
        P("seq", "head"),
        P("seq"),
        P(),
        P("head"),
        P("seq", "head"),
    )
    return jax.shard_map(
        per_device,
        mesh=mesh,
        in_specs=placed,
        out_specs=(P("seq", "head"), P("seq", "head"), P("seq", "head"), P("seq", "head")),
        check_vma=False,
    )
```
